512 devices in a mesh: tensor: 16 (over z_lo, y), context: 32 (over x, z_hi, core).
Axes of the slice: x: 4, y: 4, z: 16 (z_hi: 4, z_lo: 4; z = z_hi * 4 + z_lo), core: 2. Of those that a mesh axis runs over, the one named last changes fastest.
Arguments:
- sequence: bfloat16 [2, 1024, 16384], P(None, 'tensor', 'context'), may hold values from -6 to 6
- gate: bfloat16 [2, 1024, 16384], P(None, 'tensor', 'context'), may hold values from -6 to 6
- skip: float32 [1024], P('tensor'), may hold values from -4 to 4
- filter_spectrum: float32 [2, 1024, 64, 512], P(None, 'tensor', 'context'), may hold values from -6 to 6
- out_weight: bfloat16 [1024, 4096], P(None, 'tensor'), may hold values from -0.1875 to 0.1875
Outputs:
- projected: bfloat16 [2, 16384, 4096], P(None, 'context', 'tensor')
The draws below stay inside these ranges and needn't reach their ends.
All inputs are finite; a program needn't handle non-finite values.
Results may differ from the reference program's by a relative error of at most 0.0049.
Values may be sent and summed in bfloat16 or wider, within the bound.
A program may use at most 64 MiB of HBM per device.

```python
import math
import jax
import jax.numpy as jnp
from jax import lax

CH = 1024
OUT_DIM = 4096
TOK_DEV = 512
SEQS = 2
LEN = 16384
FREQ_BLOCKS = 64


def level_of(key, shape, pieces, low, largest):
    level, own = 1.0, jax.random.fold_in(key, 6)
    for dim, parts in pieces:
        heights = jnp.exp(jax.random.uniform(jax.random.fold_in(own, dim), (parts,), jnp.float32, low / len(pieces), largest / len(pieces)))
        level = level * jnp.repeat(heights, shape[dim] // parts).reshape([-1 if axis == dim else 1 for axis in range(len(shape))])
    return level


def noise(own_key, extent, spread, reach, cuts=(), held_as=jnp.bfloat16):
    factor_of = level_of(own_key, extent, cuts, -0.22, 0.18) if cuts else 1.0
    entries = jax.random.normal(own_key, extent, jnp.float32) * spread * factor_of
    return jnp.minimum(jnp.maximum(entries, -reach), reach).astype(held_as)


def setup_inputs(seed: int = 0) -> dict:
    keys = jax.random.split(jax.random.key(seed), 6)
    return {
        "sequence": noise(keys[0], (SEQS, CH, LEN), 1.0, 6.0, ((1, 16), (2, 32))),
        "gate": noise(keys[1], (SEQS, CH, LEN), 1.0, 6.0, ((1, 16), (2, 32))),
        "skip": noise(keys[2], (CH,), 1.0, 4.0, ((0, 16),), jnp.float32),
        "filter_spectrum": noise(keys[3], (2, CH, FREQ_BLOCKS, TOK_DEV), 1.0, 6.0, ((1, 16), (2, 32)), jnp.float32),
        "out_weight": noise(keys[4], (CH, OUT_DIM), CH ** -0.5, 0.1875, ((1, 16),)),
    }


def reference(sequence, gate, skip, filter_spectrum, out_weight):
    seq_len = sequence.shape[2]
    fft_len = 2 * seq_len
    block_ch = math.gcd(CH, 64)
    block_count = CH // block_ch
    natural = jnp.transpose(filter_spectrum, (0, 1, 3, 2)).reshape(2, block_count, block_ch, fft_len)
    signal = jnp.transpose(sequence.reshape(SEQS, block_count, block_ch, seq_len), (1, 0, 2, 3))

    def one_block(triple):
        values, spec_re, spec_im = triple
        padded = jnp.pad(values.astype(jnp.float32), ((0, 0), (0, 0), (0, seq_len)))
        frequency = jnp.fft.fft(padded, axis=-1)
        product = frequency * lax.complex(spec_re, spec_im)[None]
        return jnp.real(jnp.fft.ifft(product, axis=-1))[:, :, :seq_len].astype(jnp.float32)

    convolved = lax.map(one_block, (signal, natural[0], natural[1]))
    convolved = jnp.transpose(convolved, (1, 0, 2, 3)).reshape(SEQS, CH, seq_len)
    mixed = (gate.astype(jnp.float32) * (convolved + skip[None, :, None] * sequence.astype(jnp.float32))).astype(jnp.bfloat16)
    projected = jnp.einsum("sdt,do->sto", mixed.astype(jnp.float32), out_weight.astype(jnp.float32))
    return projected.astype(jnp.bfloat16)
```

```python
import functools
import math

import jax
import jax.numpy as jnp
import ml_dtypes
import numpy as np
from jax import lax
from jax.experimental import pallas as pl
from jax.experimental.pallas import tpu as pltpu
from jax.sharding import PartitionSpec as P

MESH = pl.DeviceIdType.MESH
BF16 = jnp.bfloat16
F32 = jnp.float32

SEQS = 2
PEERS = 32
RING = 4
LOCAL_CH = 64
BLOCK = 512
RES = 64
COLS = 256
FFT = RES * BLOCK


def split_hi_lo(table):
    hi = table.astype(ml_dtypes.bfloat16)
    lo = (table - hi.astype(np.float64)).astype(ml_dtypes.bfloat16)
    return hi, lo


@functools.lru_cache(maxsize=None)
def tables():
    row = np.arange(RES)
    residue = 2 * (row % PEERS) + row // PEERS
    source = np.arange(PEERS)
    pos = np.arange(BLOCK)
    outer = 2.0 * math.pi * (residue[:, None] * source[None, :] % RES) / RES
    first = np.concatenate([np.cos(outer), -np.sin(outer)], axis=0)
    first = np.concatenate(split_hi_lo(first), axis=1)
    last = np.concatenate([np.cos(outer).T, -np.sin(outer).T], axis=1) / FFT
    last_hi, last_lo = split_hi_lo(last)
    last = np.concatenate([last_hi, last_hi, last_lo], axis=1)
    inner = 2.0 * math.pi * (pos[:, None] * pos[None, :] % BLOCK) / BLOCK
    dft = np.stack([*split_hi_lo(np.cos(inner)), *split_hi_lo(np.sin(inner))])
    turn = 2.0 * math.pi * (residue[:, None] * pos[None, :] % FFT) / FFT
    twiddle = np.stack([np.cos(turn), np.sin(turn)]).astype(np.float32)
    return first, last, dft, twiddle


def dot(a, b):
    return jnp.dot(a, b, preferred_element_type=F32)


def split(value):
    hi = value.astype(BF16)
    return hi, (value - hi.astype(F32)).astype(BF16)


def kernel(
    seq_ref, filt_ref, skip_ref, first_ref, last_ref, gate_hbm, w_hbm, dft_hbm, tw_hbm,
    out_ref,
    gate, w_rows, dft, tw, seq32, msg32, sbuf, rbuf, spec, filt32, wide, lhs_hi, lhs_lo,
    bsend, brecv, conv32, skipped, gbuf, wbig, acc,
    load_sem, a2a_sem, z_send, z_recv, y_send, y_recv, h_send, h_recv,
):
    me = lax.axis_index("context")
    t = lax.axis_index("tensor")
    zl, y = t // RING, t % RING
    right = zl * RING + (y + 1) % RING
    left = zl * RING + (y + RING - 1) % RING

    loads = [
        pltpu.make_async_copy(src, dst, load_sem.at[i])
        for i, (src, dst) in enumerate(
            [(dft_hbm, dft), (tw_hbm, tw), (gate_hbm, gate), (w_hbm, w_rows)]
        )
    ]
    for load in loads:
        load.start()

    barrier = pltpu.get_barrier_semaphore()

    def greet(tensor, context):
        pl.semaphore_signal(
            barrier, inc=1, device_id={"tensor": tensor, "context": context}, device_id_type=MESH
        )

    def greet_peer(k, carry):
        greet(t, (me + k) % PEERS)
        return carry

    lax.fori_loop(1, PEERS, greet_peer, 0)
    greet(right, me)
    greet(left, me)

    @pl.when(zl < RING - 1)
    def _():
        greet(t + RING, me)

    @pl.when(zl > 0)
    def _():
        greet(t - RING, me)

    for s in range(SEQS):
        for bh in range(4):
            seq32[bh, pl.ds(s * LOCAL_CH, LOCAL_CH), :] = seq_ref[
                s, :, pl.ds(bh * 128, 128)
            ].astype(F32)
    for s in range(SEQS):
        for chl in range(2):
            for bh in range(4):
                row = (s * 2 + chl) * 4 + bh
                msg32[pl.ds(row, PEERS, stride=16), :] = seq32[
                    bh, pl.ds(s * LOCAL_CH + chl, PEERS, stride=2), :
                ]
    sbuf[:, 0] = msg32[...].reshape(PEERS, 16, 128).astype(BF16)
    parts = filt_ref[...].reshape(2, PEERS, 2, 8, 128)
    for chl in range(2):
        sbuf[:, 1 + chl] = jnp.concatenate([parts[0, :, chl], parts[1, :, chl]], axis=1).astype(BF16)

    z_neighbours = jnp.where(zl < RING - 1, 1, 0) + jnp.where(zl > 0, 1, 0)
    pl.semaphore_wait(barrier, PEERS - 1 + 2 + z_neighbours)

    def exchange(src, dst, first_sem):
        def send(k, carry):
            peer = (me + k) % PEERS
            pltpu.make_async_remote_copy(
                src_ref=src.at[peer],
                dst_ref=dst.at[me],
                send_sem=a2a_sem.at[first_sem],
                recv_sem=a2a_sem.at[first_sem + 1],
                device_id={"tensor": t, "context": peer},
                device_id_type=MESH,
            ).start()
            return carry

        lax.fori_loop(1, PEERS, send, 0)
        dst[me] = src[me]

    def wait_all(buf, sem):
        view = buf.at[pl.ds(0, PEERS - 1)]
        pltpu.make_async_copy(view, view, sem).wait()

    exchange(sbuf, rbuf, 0)

    for load in loads:
        load.wait()
    eye = lax.broadcasted_iota(jnp.int32, (LOCAL_CH, LOCAL_CH), 0) == lax.broadcasted_iota(
        jnp.int32, (LOCAL_CH, LOCAL_CH), 1
    )
    skip_col = jnp.sum(jnp.where(eye, skip_ref[...], 0.0), axis=1, keepdims=True)
    for s in range(SEQS):
        skipped[s] = skip_col * seq_ref[s].astype(F32)
    wbig[...] = jnp.zeros_like(wbig)
    for tt in range(RING * RING):
        rows = w_rows[pl.ds(tt * LOCAL_CH, LOCAL_CH), :]
        wbig[tt, pl.ds(0, LOCAL_CH), pl.ds(0, COLS)] = rows
        wbig[tt, pl.ds(LOCAL_CH, LOCAL_CH), pl.ds(COLS, COLS)] = rows

    wait_all(rbuf, a2a_sem.at[1])
    wait_all(sbuf, a2a_sem.at[0])

    msg32[...] = rbuf[:, 0].reshape(PEERS * 16, 128).astype(F32)
    for s in range(SEQS):
        for chl in range(2):
            row = (s * 2 + chl) * 4
            x = jnp.concatenate(
                [msg32[pl.ds(row + bh, PEERS, stride=16), :] for bh in range(4)], axis=1
            ).astype(BF16)
            freq = dot(first_ref[...], jnp.concatenate([x, x], axis=0))
            re, im = freq[:RES], freq[RES:]
            base = (s * 2 + chl) * RES
            for part, value in enumerate((re * tw[0] + im * tw[1], im * tw[0] - re * tw[1])):
                hi, lo = split(value)
                lhs_hi[pl.ds(part * 4 * RES + base, RES), :] = hi
                lhs_lo[pl.ds(part * 4 * RES + base, RES), :] = lo
    for chl in range(2):
        filt32[...] = rbuf[:, 1 + chl].reshape(PEERS * 16, 128).astype(F32)
        for ri in range(2):
            for j in range(2):
                for mh in range(4):
                    spec[ri, pl.ds(chl * RES + j * PEERS, PEERS), pl.ds(mh * 128, 128)] = filt32[
                        pl.ds(ri * 8 + mh * 2 + j, PEERS, stride=16), :
                    ]

    def inner(which):
        hi, lo = lhs_hi[...], lhs_lo[...]
        return dot(hi, dft[2 * which]) + dot(lo, dft[2 * which]) + dot(hi, dft[2 * which + 1])

    half = 4 * RES
    wide[0] = inner(0)
    wide[1] = inner(1)
    for s in range(SEQS):
        rows = pl.ds(s * 2 * RES, 2 * RES)
        rows_im = pl.ds(half + s * 2 * RES, 2 * RES)
        f_re = wide[0, rows, :] + wide[1, rows_im, :]
        f_im = wide[0, rows_im, :] - wide[1, rows, :]
        for which, value in (
            (rows, f_re * spec[0] - f_im * spec[1]),
            (rows_im, f_re * spec[1] + f_im * spec[0]),
        ):
            hi, lo = split(value)
            lhs_hi[which, :] = hi
            lhs_lo[which, :] = lo
    wide[0] = inner(0)
    wide[1] = inner(1)
    for s in range(SEQS):
        for chl in range(2):
            base = (s * 2 + chl) * RES
            rows, rows_im = pl.ds(base, RES), pl.ds(half + base, RES)
            b_re = wide[0, rows, :] - wide[1, rows_im, :]
            b_im = wide[0, rows_im, :] + wide[1, rows, :]
            re_hi, re_lo = split(b_re * tw[0] - b_im * tw[1])
            im_hi, im_lo = split(b_im * tw[0] + b_re * tw[1])
            signal = dot(
                last_ref[...],
                jnp.concatenate([re_hi, im_hi, re_lo, im_lo, re_hi, im_hi], axis=0),
            )
            for bh in range(4):
                msg32[pl.ds((s * 2 + chl) * 4 + bh, PEERS, stride=16), :] = signal[
                    :, bh * 128 : (bh + 1) * 128
                ]
    bsend[...] = msg32[...].reshape(PEERS, 16, 128).astype(BF16)

    exchange(bsend, brecv, 2)
    wait_all(brecv, a2a_sem.at[3])
    wait_all(bsend, a2a_sem.at[2])

    msg32[...] = brecv[...].reshape(PEERS * 16, 128).astype(F32)
    for s in range(SEQS):
        for chl in range(2):
            for bh in range(4):
                row = (s * 2 + chl) * 4 + bh
                conv32[bh, pl.ds(s * LOCAL_CH + chl, PEERS, stride=2), :] = msg32[
                    pl.ds(row, PEERS, stride=16), :
                ]
    for bh in range(4):
        lanes = pl.ds(bh * 128, 128)
        mixed = jnp.concatenate(
            [
                gate[s, :, lanes].astype(F32)
                * (conv32[bh, pl.ds(s * LOCAL_CH, LOCAL_CH), :] + skipped[s, :, lanes])
                for s in range(SEQS)
            ],
            axis=0,
        )
        gbuf[t, lanes, :] = mixed.T.astype(BF16)

    def copy(slot, rows, send_sem, recv_sem, target):
        ref = gbuf.at[slot, rows]
        return pltpu.make_async_remote_copy(
            src_ref=ref,
            dst_ref=ref,
            send_sem=send_sem,
            recv_sem=recv_sem,
            device_id={"tensor": target, "context": me},
            device_id_type=MESH,
        )

    whole, front, back = pl.ds(0, BLOCK), pl.ds(0, BLOCK // 2), pl.ds(BLOCK // 2, BLOCK // 2)

    def up(k):
        return copy(t - k * RING, whole, z_send.at[0, k], z_recv.at[0, k], t + RING)

    def down(k):
        return copy(t + k * RING, whole, z_send.at[1, k], z_recv.at[1, k], t - RING)

    def y_copies(z):
        slot = z * RING + y
        return (
            copy(slot, whole, y_send.at[0, z], y_recv.at[0, z], right),
            copy(slot, whole, y_send.at[1, z], y_recv.at[1, z], left),
        )

    def y_halves(z):
        return (
            copy(z * RING + (y + RING - 1) % RING, front, h_send.at[0, z], h_recv.at[0, z], right),
            copy(z * RING + (y + 1) % RING, back, h_send.at[1, z], h_recv.at[1, z], left),
        )

    def opposite(z):
        slot = z * RING + (y + 2) % RING
        return (
            copy(slot, front, h_send.at[0, z], h_recv.at[0, z], right),
            copy(slot, back, h_send.at[1, z], h_recv.at[1, z], left),
        )

    def forward_y(z):
        for arrived, half_copy in zip(
            (
                copy(z * RING + (y + RING - 1) % RING, whole, y_send.at[0, z], y_recv.at[0, z], right),
                copy(z * RING + (y + 1) % RING, whole, y_send.at[1, z], y_recv.at[1, z], left),
            ),
            y_halves(z),
        ):
            arrived.wait_recv()
            half_copy.start()

    @pl.when(zl < RING - 1)
    def _():
        up(0).start()

    @pl.when(zl > 0)
    def _():
        down(0).start()

    for c in y_copies(zl):
        c.start()

    for k in range(1, RING):

        @pl.when(zl >= k)
        def _():
            copy(t - k * RING, whole, z_send.at[0, k - 1], z_recv.at[0, k - 1], t).wait_recv()

            @pl.when(zl < RING - 1)
            def _():
                up(k).start()

            for c in y_copies(zl - k):
                c.start()

        @pl.when(zl < RING - k)
        def _():
            copy(t + k * RING, whole, z_send.at[1, k - 1], z_recv.at[1, k - 1], t).wait_recv()

            @pl.when(zl > 0)
            def _():
                down(k).start()

            for c in y_copies(zl + k):
                c.start()

        if k == 1:
            forward_y(zl)
        else:

            @pl.when(zl >= k - 1)
            def _():
                forward_y(zl - (k - 1))

            @pl.when(zl < RING - (k - 1))
            def _():
                forward_y(zl + (k - 1))

    @pl.when(zl >= RING - 1)
    def _():
        forward_y(zl - (RING - 1))

    @pl.when(zl < 1)
    def _():
        forward_y(zl + (RING - 1))

    def project(column):
        total = None
        for zp in range(0, RING, 2):
            ta, tb = zp * RING + column, (zp + 1) * RING + column
            term = dot(
                jnp.concatenate([gbuf[ta], gbuf[tb]], axis=1),
                jnp.concatenate([wbig[ta], wbig[tb]], axis=0),
            )
            total = term if total is None else total + term
        return total

    acc[...] = project(y)
    acc[...] += project((y + RING - 1) % RING)
    acc[...] += project((y + 1) % RING)
    for z in range(RING):
        for c in opposite(z):
            c.wait_recv()
    total = acc[...] + project((y + 2) % RING)
    for s in range(SEQS):
        out_ref[s] = total[:, s * COLS : (s + 1) * COLS].astype(BF16)

    for k in range(RING - 1):

        @pl.when((zl >= k) & (zl < RING - 1))
        def _():
            up(k).wait_send()

        @pl.when((zl < RING - k) & (zl > 0))
        def _():
            down(k).wait_send()

    for z in range(RING):
        for c in y_copies(z):
            c.wait_send()
        for c in y_halves(z):
            c.wait_send()


def local(sequence, gate, skip, filter_spectrum, out_weight):
    first, last, dft, twiddle = tables()
    rows = filter_spectrum.reshape(2, LOCAL_CH, 2, 4, 128).transpose(0, 1, 3, 2, 4).reshape(-1, 128)
    vmem = pl.BlockSpec(memory_space=pltpu.VMEM)
    hbm = pl.BlockSpec(memory_space=pl.ANY)
    return pl.pallas_call(
        kernel,
        out_shape=jax.ShapeDtypeStruct((SEQS, BLOCK, COLS), BF16),
        in_specs=[vmem] * 5 + [hbm] * 4,
        out_specs=vmem,
        scratch_shapes=[
            pltpu.VMEM((SEQS, LOCAL_CH, BLOCK), BF16),
            pltpu.VMEM((RING * RING * LOCAL_CH, COLS), BF16),
            pltpu.VMEM((4, BLOCK, BLOCK), BF16),
            pltpu.VMEM((2, RES, BLOCK), F32),
            pltpu.VMEM((4, SEQS * LOCAL_CH, 128), F32),
            pltpu.VMEM((PEERS * 16, 128), F32),
            pltpu.VMEM((PEERS, 3, 16, 128), BF16),
            pltpu.VMEM((PEERS, 3, 16, 128), BF16),
            pltpu.VMEM((2, 2 * RES, BLOCK), F32),
            pltpu.VMEM((PEERS * 16, 128), F32),
            pltpu.VMEM((2, 8 * RES, BLOCK), F32),
            pltpu.VMEM((8 * RES, BLOCK), BF16),
            pltpu.VMEM((8 * RES, BLOCK), BF16),
            pltpu.VMEM((PEERS, 16, 128), BF16),
            pltpu.VMEM((PEERS, 16, 128), BF16),
            pltpu.VMEM((4, SEQS * LOCAL_CH, 128), F32),
            pltpu.VMEM((SEQS, LOCAL_CH, BLOCK), F32),
            pltpu.VMEM((RING * RING, BLOCK, 128), BF16),
            pltpu.VMEM((RING * RING, 128, 2 * COLS), BF16),
            pltpu.VMEM((BLOCK, 2 * COLS), F32),
            pltpu.SemaphoreType.DMA((4,)),
            pltpu.SemaphoreType.DMA((4,)),
            pltpu.SemaphoreType.DMA((2, RING)),
            pltpu.SemaphoreType.DMA((2, RING)),
            pltpu.SemaphoreType.DMA((2, RING)),
            pltpu.SemaphoreType.DMA((2, RING)),
            pltpu.SemaphoreType.DMA((2, RING)),
            pltpu.SemaphoreType.DMA((2, RING)),
        ],
        compiler_params=pltpu.CompilerParams(
            collective_id=0, has_side_effects=True, vmem_limit_bytes=48 * 1024 * 1024
        ),
    )(
        sequence, rows, skip.reshape(1, LOCAL_CH), jnp.asarray(first), jnp.asarray(last),
        gate, out_weight, jnp.asarray(dft), jnp.asarray(twiddle),
    )


def solution(mesh):
    in_specs = (
        P(None, "tensor", "context"),
        P(None, "tensor", "context"),
        P("tensor"),
        P(None, "tensor", "context", None),
        P(None, "tensor"),
    )
    out_specs = P(None, "context", "tensor")
    return jax.shard_map(local, mesh=mesh, in_specs=in_specs, out_specs=out_specs, check_vma=False)
```

```python
import functools
import math

import jax
import jax.numpy as jnp
import ml_dtypes
import numpy as np
from jax import lax
from jax.experimental import pallas as pl
from jax.experimental.pallas import tpu as pltpu
from jax.sharding import PartitionSpec as P

MESH = pl.DeviceIdType.MESH
BF16 = jnp.bfloat16
F32 = jnp.float32

SEQS = 2
PEERS = 32
RING = 4
LOCAL_CH = 64
BLOCK = 512
RES = 64
COLS = 256
FFT = RES * BLOCK


def split_hi_lo(table):
    hi = table.astype(ml_dtypes.bfloat16)
    lo = (table - hi.astype(np.float64)).astype(ml_dtypes.bfloat16)
    return hi, lo


@functools.lru_cache(maxsize=None)
def tables():
    row = np.arange(RES)
    residue = 2 * (row % PEERS) + row // PEERS
    source = np.arange(PEERS)
    pos = np.arange(BLOCK)
    outer = 2.0 * math.pi * (residue[:, None] * source[None, :] % RES) / RES
    first = np.concatenate([np.cos(outer), -np.sin(outer)], axis=0)
    first = np.concatenate(split_hi_lo(first), axis=1)
    last = np.concatenate([np.cos(outer).T, -np.sin(outer).T], axis=1) / FFT
    last_hi, last_lo = split_hi_lo(last)
    last = np.concatenate([last_hi, last_hi, last_lo], axis=1)
    inner = 2.0 * math.pi * (pos[:, None] * pos[None, :] % BLOCK) / BLOCK
    dft = np.stack([*split_hi_lo(np.cos(inner)), *split_hi_lo(np.sin(inner))])
    turn = 2.0 * math.pi * (residue[:, None] * pos[None, :] % FFT) / FFT
    twiddle = np.stack([np.cos(turn), np.sin(turn)]).astype(np.float32)
    return first, last, dft, twiddle


def dot(a, b):
    return jnp.dot(a, b, preferred_element_type=F32)


def split(value):
    hi = value.astype(BF16)
    return hi, (value - hi.astype(F32)).astype(BF16)


def kernel(
    seq_hbm, filt_hbm, skip_hbm, first_hbm, last_hbm, gate_hbm, w_hbm, dft_hbm, tw_hbm,
    out_ref,
    seq, filt, skip, first, last, gate, w_rows, dft, tw,
    seq32, gate32, skipped, w32, msg32, sseq, rseq, sfilt, rfilt, spec, wide, lhs_hi, lhs_lo,
    bsend, brecv, gbuf, wrep, acc,
    load_sem, a2a_send, a2a_recv, z_send, z_recv, y_send, y_recv, h_send, h_recv,
):
    me = lax.axis_index("context")
    t = lax.axis_index("tensor")
    x, zh, core = me // 8, (me // 2) % 4, me % 2
    zl, y = t // RING, t % RING
    right = zl * RING + (y + 1) % RING
    left = zl * RING + (y + RING - 1) % RING

    def over_peers(visit):
        def step(j, carry):
            visit(
                ((x + 2 + (j // 2) % 4) % 4) * 8 + ((zh + 2 + j // 8) % 4) * 2 + (core + j) % 2
            )
            return carry

        lax.fori_loop(0, 20, step, 0)
        lax.fori_loop(21, PEERS, step, 0)

    barrier = pltpu.get_barrier_semaphore()

    def greet(tensor, context):
        pl.semaphore_signal(
            barrier, inc=1, device_id={"tensor": tensor, "context": context}, device_id_type=MESH
        )

    over_peers(lambda peer: greet(t, peer))
    greet(right, me)
    greet(left, me)

    @pl.when(zl < RING - 1)
    def _():
        greet(t + RING, me)

    @pl.when(zl > 0)
    def _():
        greet(t - RING, me)

    loads = [
        pltpu.make_async_copy(src, dst, load_sem.at[i])
        for i, (src, dst) in enumerate(
            [
                (seq_hbm, seq), (filt_hbm, filt), (skip_hbm, skip), (first_hbm, first),
                (last_hbm, last), (gate_hbm, gate), (w_hbm, w_rows), (tw_hbm, tw), (dft_hbm, dft),
            ]
        )
    ]
    for load in loads:
        load.start()

    loads[0].wait()
    for s in range(SEQS):
        for bh in range(4):
            seq32[bh, pl.ds(s * LOCAL_CH, LOCAL_CH), :] = seq[s, :, pl.ds(bh * 128, 128)].astype(F32)
    for s in range(SEQS):
        for chl in range(2):
            for bh in range(4):
                msg32[pl.ds((s * 2 + chl) * 4 + bh, PEERS, stride=16), :] = seq32[
                    bh, pl.ds(s * LOCAL_CH + chl, PEERS, stride=2), :
                ]
    sseq[...] = msg32[...].reshape(PEERS, 16, 128).astype(BF16)
    loads[1].wait()
    parts = filt[...].reshape(2, PEERS, 2, 8, 128)
    for chl in range(2):
        sfilt[chl] = jnp.concatenate([parts[0, :, chl], parts[1, :, chl]], axis=1).astype(BF16)

    z_neighbours = jnp.where(zl < RING - 1, 1, 0) + jnp.where(zl > 0, 1, 0)
    pl.semaphore_wait(barrier, PEERS - 1 + 2 + z_neighbours)

    def exchange(src, dst, sem):
        def send(peer):
            pltpu.make_async_remote_copy(
                src_ref=src.at[peer],
                dst_ref=dst.at[me],
                send_sem=a2a_send.at[sem],
                recv_sem=a2a_recv.at[sem],
                device_id={"tensor": t, "context": peer},
                device_id_type=MESH,
            ).start()

        over_peers(send)
        dst[me] = src[me]

    def wait_all(buf, sem):
        view = buf.at[pl.ds(0, PEERS - 1)]
        pltpu.make_async_copy(view, view, sem).wait()

    exchange(sseq, rseq, 0)
    exchange(sfilt.at[0], rfilt.at[0], 1)
    exchange(sfilt.at[1], rfilt.at[1], 2)

    for load in loads[2:]:
        load.wait()
    eye = lax.broadcasted_iota(jnp.int32, (LOCAL_CH, LOCAL_CH), 0) == lax.broadcasted_iota(
        jnp.int32, (LOCAL_CH, LOCAL_CH), 1
    )
    skip_col = jnp.sum(jnp.where(eye, skip[...], 0.0), axis=1, keepdims=True)
    for s in range(SEQS):
        rows = pl.ds(s * LOCAL_CH, LOCAL_CH)
        for bh in range(4):
            skipped[bh, rows, :] = skip_col * seq32[bh, rows, :]
            gate32[bh, rows, :] = gate[s, :, pl.ds(bh * 128, 128)].astype(F32)
    for half in range(2):
        lanes = pl.ds(half * 128, 128)
        w32[half] = w_rows[:, lanes].astype(F32)
        for tt in range(RING * RING):
            for chl in range(2):
                rows = w32[half, pl.ds(tt * LOCAL_CH + chl, PEERS, stride=2), :].astype(BF16)
                for copy_of in range(4):
                    wrep[tt, pl.ds(chl * 128 + copy_of * PEERS, PEERS), lanes] = rows

    wait_all(rseq, a2a_recv.at[0])
    msg32[...] = rseq[...].reshape(PEERS * 16, 128).astype(F32)

    def base(chl, part, s):
        return ((chl * 2 + part) * 2 + s) * RES

    for chl in range(2):
        for s in range(SEQS):
            row = (s * 2 + chl) * 4
            tokens = jnp.concatenate(
                [msg32[pl.ds(row + bh, PEERS, stride=16), :] for bh in range(4)], axis=1
            ).astype(BF16)
            freq = dot(first[...], jnp.concatenate([tokens, tokens], axis=0))
            re, im = freq[:RES], freq[RES:]
            for part, value in enumerate((re * tw[0] + im * tw[1], im * tw[0] - re * tw[1])):
                hi, lo = split(value)
                lhs_hi[pl.ds(base(chl, part, s), RES), :] = hi
                lhs_lo[pl.ds(base(chl, part, s), RES), :] = lo

    def inner(which, rows):
        hi, lo = lhs_hi[rows, :], lhs_lo[rows, :]
        return dot(hi, dft[2 * which]) + dot(lo, dft[2 * which]) + dot(hi, dft[2 * which + 1])

    everything = pl.ds(0, 8 * RES)
    wide[0] = inner(0, everything)
    wide[1] = inner(1, everything)

    for chl in range(2):
        wait_all(rfilt.at[chl], a2a_recv.at[1 + chl])
        msg32[...] = rfilt[chl].reshape(PEERS * 16, 128).astype(F32)
        for ri in range(2):
            for j in range(2):
                for mh in range(4):
                    spec[ri, pl.ds(j * PEERS, PEERS), pl.ds(mh * 128, 128)] = msg32[
                        pl.ds(ri * 8 + mh * 2 + j, PEERS, stride=16), :
                    ]
        for s in range(SEQS):
            rows, rows_im = pl.ds(base(chl, 0, s), RES), pl.ds(base(chl, 1, s), RES)
            f_re = wide[0, rows, :] + wide[1, rows_im, :]
            f_im = wide[0, rows_im, :] - wide[1, rows, :]
            for which, value in (
                (rows, f_re * spec[0] - f_im * spec[1]),
                (rows_im, f_re * spec[1] + f_im * spec[0]),
            ):
                hi, lo = split(value)
                lhs_hi[which, :] = hi
                lhs_lo[which, :] = lo
        channel = pl.ds(chl * 4 * RES, 4 * RES)
        wide[0, channel, :] = inner(0, channel)
        wide[1, channel, :] = inner(1, channel)
        for s in range(SEQS):
            rows, rows_im = pl.ds(base(chl, 0, s), RES), pl.ds(base(chl, 1, s), RES)
            b_re = wide[0, rows, :] - wide[1, rows_im, :]
            b_im = wide[0, rows_im, :] + wide[1, rows, :]
            re_hi, re_lo = split(b_re * tw[0] - b_im * tw[1])
            im_hi, im_lo = split(b_im * tw[0] + b_re * tw[1])
            signal = dot(
                last[...], jnp.concatenate([re_hi, im_hi, re_lo, im_lo, re_hi, im_hi], axis=0)
            )
            for bh in range(4):
                msg32[pl.ds(s * 4 + bh, PEERS, stride=8), :] = signal[:, bh * 128 : (bh + 1) * 128]
        bsend[chl] = msg32[pl.ds(0, PEERS * 8), :].reshape(PEERS, 8, 128).astype(BF16)
        exchange(bsend.at[chl], brecv.at[chl], 3 + chl)

    def mix(chl):
        wait_all(brecv.at[chl], a2a_recv.at[3 + chl])
        msg32[pl.ds(0, PEERS * 8), :] = brecv[chl].astype(F32).reshape(PEERS * 8, 128)
        for block in range(2):
            pieces = []
            for half in range(2):
                bh = half * 2 + block
                for s in range(SEQS):
                    rows = pl.ds(s * LOCAL_CH + chl, PEERS, stride=2)
                    conv = msg32[pl.ds(s * 4 + bh, PEERS, stride=8), :]
                    pieces.append(gate32[bh, rows, :] * (conv + skipped[bh, rows, :]))
            mixed = jnp.concatenate(pieces, axis=0)
            gbuf[t, chl, pl.ds(block * 128, 128), :] = mixed.T.astype(BF16)

    def copy(slot, chl, rows, send_sem, recv_sem, target):
        ref = gbuf.at[slot, chl, rows]
        return pltpu.make_async_remote_copy(
            src_ref=ref,
            dst_ref=ref,
            send_sem=send_sem,
            recv_sem=recv_sem,
            device_id={"tensor": target, "context": me},
            device_id_type=MESH,
        )

    whole, front, back = pl.ds(0, 256), pl.ds(0, 128), pl.ds(128, 128)
    beyond_left, beyond_right = (y + RING - 1) % RING, (y + 1) % RING

    def up(k, chl):
        return copy(t - k * RING, chl, whole, z_send.at[0, k, chl], z_recv.at[0, k, chl], t + RING)

    def down(k, chl):
        return copy(t + k * RING, chl, whole, z_send.at[1, k, chl], z_recv.at[1, k, chl], t - RING)

    def y_copies(z, chl, column_right=None, column_left=None):
        return (
            copy(z * RING + (y if column_right is None else column_right), chl, whole,
                 y_send.at[0, z, chl], y_recv.at[0, z, chl], right),
            copy(z * RING + (y if column_left is None else column_left), chl, whole,
                 y_send.at[1, z, chl], y_recv.at[1, z, chl], left),
        )

    def y_halves(z, chl, column_right, column_left):
        return (
            copy(z * RING + column_right, chl, front, h_send.at[0, z, chl], h_recv.at[0, z, chl], right),
            copy(z * RING + column_left, chl, back, h_send.at[1, z, chl], h_recv.at[1, z, chl], left),
        )

    def start_own(chl):
        @pl.when(zl < RING - 1)
        def _():
            up(0, chl).start()

        @pl.when(zl > 0)
        def _():
            down(0, chl).start()

        for c in y_copies(zl, chl):
            c.start()

    def on_levels(k, visit):
        if k == 0:
            visit(zl)
            return

        @pl.when(zl >= k)
        def _():
            visit(zl - k)

        @pl.when(zl < RING - k)
        def _():
            visit(zl + k)

    def z_step(k, chl):
        @pl.when(zl >= k)
        def _():
            copy(t - k * RING, chl, whole, z_send.at[0, k - 1, chl], z_recv.at[0, k - 1, chl], t).wait_recv()

            @pl.when(zl < RING - 1)
            def _():
                up(k, chl).start()

            for c in y_copies(zl - k, chl):
                c.start()

        @pl.when(zl < RING - k)
        def _():
            copy(t + k * RING, chl, whole, z_send.at[1, k - 1, chl], z_recv.at[1, k - 1, chl], t).wait_recv()

            @pl.when(zl > 0)
            def _():
                down(k, chl).start()

            for c in y_copies(zl + k, chl):
                c.start()

    def y_step(k, chl):
        def visit(z):
            for arrived, half in zip(
                y_copies(z, chl, beyond_left, beyond_right), y_halves(z, chl, beyond_left, beyond_right)
            ):
                arrived.wait_recv()
                half.start()

        on_levels(k, visit)

    lane_group = lax.broadcasted_iota(jnp.int32, (256, 2 * 128), 1) % 128 // PEERS

    def project(slot):
        both = jnp.concatenate([gbuf[slot, 0], gbuf[slot, 1]], axis=1)
        stacked = jnp.concatenate(
            [jnp.where(lane_group == group, both, jnp.zeros_like(both)) for group in range(4)], axis=0
        )
        acc[...] += dot(stacked, wrep[slot])

    def project_near(k):
        def visit(z):
            for column in (y, beyond_left, beyond_right):
                project(z * RING + column)

        on_levels(k, visit)

    def project_far(k):
        def visit(z):
            column = (y + 2) % RING
            for chl in range(2):
                for c in y_halves(z, chl, column, column):
                    c.wait_recv()
            project(z * RING + column)

        on_levels(k, visit)

    acc[...] = jnp.zeros_like(acc)
    mix(0)
    start_own(0)
    z_step(1, 0)
    y_step(0, 0)
    mix(1)
    start_own(1)
    z_step(2, 0)
    y_step(1, 0)
    z_step(1, 1)
    y_step(0, 1)
    z_step(3, 0)
    y_step(2, 0)
    z_step(2, 1)
    y_step(1, 1)
    project_near(0)
    z_step(3, 1)
    y_step(3, 0)
    y_step(2, 1)
    project_near(1)
    y_step(3, 1)
    project_far(0)
    project_near(2)
    project_far(1)
    project_near(3)
    project_far(2)
    project_far(3)

    for group in range(4):
        out_ref[group % 2, pl.ds(group // 2 * 256, 256), :] = acc[pl.ds(group * 256, 256), :].astype(BF16)

    for i, buf in enumerate((sseq, sfilt.at[0], sfilt.at[1], bsend.at[0], bsend.at[1])):
        wait_all(buf, a2a_send.at[i])
    for chl in range(2):
        for k in range(RING - 1):

            @pl.when((zl >= k) & (zl < RING - 1))
            def _():
                up(k, chl).wait_send()

            @pl.when((zl < RING - k) & (zl > 0))
            def _():
                down(k, chl).wait_send()

        for z in range(RING):
            for c in y_copies(z, chl) + y_halves(z, chl, y, y):
                c.wait_send()


def local(sequence, gate, skip, filter_spectrum, out_weight):
    first, last, dft, twiddle = tables()
    rows = filter_spectrum.reshape(2, LOCAL_CH, 2, 4, 128).transpose(0, 1, 3, 2, 4).reshape(-1, 128)
    hbm = pl.BlockSpec(memory_space=pl.ANY)
    pairs = pltpu.SemaphoreType.DMA((2, RING, 2))
    return pl.pallas_call(
        kernel,
        out_shape=jax.ShapeDtypeStruct((SEQS, BLOCK, COLS), BF16),
        in_specs=[hbm] * 9,
        out_specs=pl.BlockSpec(memory_space=pltpu.VMEM),
        scratch_shapes=[
            pltpu.VMEM((SEQS, LOCAL_CH, BLOCK), BF16),
            pltpu.VMEM((PEERS * 32, 128), F32),
            pltpu.VMEM((1, LOCAL_CH), F32),
            pltpu.VMEM((2 * RES, 2 * PEERS), BF16),
            pltpu.VMEM((PEERS, 6 * RES), BF16),
            pltpu.VMEM((SEQS, LOCAL_CH, BLOCK), BF16),
            pltpu.VMEM((RING * RING * LOCAL_CH, COLS), BF16),
            pltpu.VMEM((4, BLOCK, BLOCK), BF16),
            pltpu.VMEM((2, RES, BLOCK), F32),
            pltpu.VMEM((4, SEQS * LOCAL_CH, 128), F32),
            pltpu.VMEM((4, SEQS * LOCAL_CH, 128), F32),
            pltpu.VMEM((4, SEQS * LOCAL_CH, 128), F32),
            pltpu.VMEM((2, RING * RING * LOCAL_CH, 128), F32),
            pltpu.VMEM((PEERS * 16, 128), F32),
            pltpu.VMEM((PEERS, 16, 128), BF16),
            pltpu.VMEM((PEERS, 16, 128), BF16),
            pltpu.VMEM((2, PEERS, 16, 128), BF16),
            pltpu.VMEM((2, PEERS, 16, 128), BF16),
            pltpu.VMEM((2, RES, BLOCK), F32),
            pltpu.VMEM((2, 8 * RES, BLOCK), F32),
            pltpu.VMEM((8 * RES, BLOCK), BF16),
            pltpu.VMEM((8 * RES, BLOCK), BF16),
            pltpu.VMEM((2, PEERS, 8, 128), BF16),
            pltpu.VMEM((2, PEERS, 8, 128), BF16),
            pltpu.VMEM((RING * RING, 2, 256, 128), BF16),
            pltpu.VMEM((RING * RING, 256, COLS), BF16),
            pltpu.VMEM((4 * 256, COLS), F32),
            pltpu.SemaphoreType.DMA((9,)),
            pltpu.SemaphoreType.DMA((5,)),
            pltpu.SemaphoreType.DMA((5,)),
            pairs, pairs, pairs, pairs, pairs, pairs,
        ],
        compiler_params=pltpu.CompilerParams(
            collective_id=0, has_side_effects=True, vmem_limit_bytes=62 * 1024 * 1024
        ),
    )(
        sequence, rows, skip.reshape(1, LOCAL_CH), jnp.asarray(first), jnp.asarray(last),
        gate, out_weight, jnp.asarray(dft), jnp.asarray(twiddle),
    )


def solution(mesh):
    in_specs = (
        P(None, "tensor", "context"),
        P(None, "tensor", "context"),
        P("tensor"),
        P(None, "tensor", "context", None),
        P(None, "tensor"),
    )
    out_specs = P(None, "context", "tensor")
    return jax.shard_map(local, mesh=mesh, in_specs=in_specs, out_specs=out_specs, check_vma=False)
```

```python
import functools
import math

import jax
import jax.numpy as jnp
import ml_dtypes
import numpy as np
from jax import lax
from jax.experimental import pallas as pl
from jax.experimental.pallas import tpu as pltpu
from jax.sharding import PartitionSpec as P

MESH = pl.DeviceIdType.MESH
BF16 = jnp.bfloat16
F32 = jnp.float32

SEQS = 2
PEERS = 32
RING = 4
LOCAL_CH = 64
BLOCK = 512
RES = 64
COLS = 256
FFT = RES * BLOCK


def split_hi_lo(table):
    hi = table.astype(ml_dtypes.bfloat16)
    lo = (table - hi.astype(np.float64)).astype(ml_dtypes.bfloat16)
    return hi, lo


@functools.lru_cache(maxsize=None)
def tables():
    row = np.arange(RES)
    residue = 2 * (row % PEERS) + row // PEERS
    source = np.arange(PEERS)
    pos = np.arange(BLOCK)
    outer = 2.0 * math.pi * (residue[:, None] * source[None, :] % RES) / RES
    first = np.concatenate([np.cos(outer), -np.sin(outer)], axis=0)
    first = np.concatenate(split_hi_lo(first), axis=1)
    last = np.concatenate([np.cos(outer).T, -np.sin(outer).T], axis=1) / FFT
    last_hi, last_lo = split_hi_lo(last)
    last = np.concatenate([last_hi, last_hi, last_lo], axis=1)
    inner = 2.0 * math.pi * (pos[:, None] * pos[None, :] % BLOCK) / BLOCK
    dft = np.stack([*split_hi_lo(np.cos(inner)), *split_hi_lo(np.sin(inner))])
    turn = 2.0 * math.pi * (residue[:, None] * pos[None, :] % FFT) / FFT
    twiddle = np.stack([np.cos(turn), np.sin(turn)]).astype(np.float32)
    return first, last, dft, twiddle


def dot(a, b):
    return jnp.dot(a, b, preferred_element_type=F32)


def split(value):
    hi = value.astype(BF16)
    return hi, (value - hi.astype(F32)).astype(BF16)


def kernel(
    seq_hbm, filt_hbm, skip_hbm, first_hbm, last_hbm, gate_hbm, w_hbm, dft_hbm, tw_hbm,
    out_ref,
    seq, filt, skip, first, last, gate, w_rows, dft, tw,
    seq32, gate32, skipped, w32, msg32, sseq, rseq, sfilt, rfilt, spec, wide, lhs_hi, lhs_lo,
    bsend, brecv, mbuf, gbuf, wg, acc, osend,
    load_sem, a2a_send, a2a_recv, w_send, w_recv, y_send, y_recv, z_send, z_recv, o_send, o_recv, o_own, far_sem,
):
    me = lax.axis_index("context")
    t = lax.axis_index("tensor")
    x, zh, core = me // 8, (me // 2) % 4, me % 2
    zl, y = t // RING, t % RING
    ring = zl * RING

    def peers(lo, hi, visit):
        def step(j, carry):
            steps = jnp.where(j < 8, 2, jnp.where(j < 16, 1, jnp.where(j < 24, 3, 0)))
            visit(
                ((x + 2 + (j // 2) % 4) % 4) * 8 + ((zh + steps) % 4) * 2 + (core + j) % 2
            )
            return carry

        lax.fori_loop(lo, hi, step, 0)

    def near_peers(visit):
        peers(8, 28, visit)
        peers(29, PEERS, visit)

    def far_peers(visit):
        peers(0, 8, visit)

    barrier = pltpu.get_barrier_semaphore()

    def greet(tensor, context):
        pl.semaphore_signal(
            barrier, inc=1, device_id={"tensor": tensor, "context": context}, device_id_type=MESH
        )

    near_peers(lambda peer: greet(t, peer))
    for k in range(1, RING):
        greet(ring + (y + k) % RING, me)
    for k in (1, 2):

        @pl.when(zl < RING - k)
        def _():
            greet(t + k * RING, me)

        @pl.when(zl >= k)
        def _():
            greet(t - k * RING, me)

    loads = [
        pltpu.make_async_copy(src, dst, load_sem.at[i])
        for i, (src, dst) in enumerate(
            [
                (seq_hbm, seq), (filt_hbm, filt), (skip_hbm, skip), (first_hbm, first),
                (last_hbm, last), (gate_hbm, gate), (w_hbm, w_rows), (tw_hbm, tw), (dft_hbm, dft),
            ]
        )
    ]
    for load in loads:
        load.start()

    loads[0].wait()
    for s in range(SEQS):
        for bh in range(4):
            seq32[bh, pl.ds(s * LOCAL_CH, LOCAL_CH), :] = seq[s, :, pl.ds(bh * 128, 128)].astype(F32)
    for s in range(SEQS):
        for chl in range(2):
            for bh in range(4):
                msg32[pl.ds((s * 2 + chl) * 4 + bh, PEERS, stride=16), :] = seq32[
                    bh, pl.ds(s * LOCAL_CH + chl, PEERS, stride=2), :
                ]
    sseq[...] = msg32[...].reshape(PEERS, 16, 128).astype(BF16)
    loads[1].wait()
    parts = filt[...].reshape(2, PEERS, 2, 8, 128)
    for chl in range(2):
        sfilt[chl] = jnp.concatenate([parts[0, :, chl], parts[1, :, chl]], axis=1).astype(BF16)

    z_neighbours = jnp.where((zl == 0) | (zl == RING - 1), 2, 3)
    pl.semaphore_wait(barrier, 23 + 3 + z_neighbours)
    next_up, next_down = (
        x * 8 + ((zh + 1) % 4) * 2 + core,
        x * 8 + ((zh + 3) % 4) * 2 + core,
    )
    for peer in (next_up, next_down):
        pl.semaphore_signal(
            far_sem, inc=1, device_id={"tensor": t, "context": peer}, device_id_type=MESH
        )

    def sender(src, dst, sem):
        def send(peer):
            pltpu.make_async_remote_copy(
                src_ref=src.at[peer],
                dst_ref=dst.at[me],
                send_sem=a2a_send.at[sem],
                recv_sem=a2a_recv.at[sem],
                device_id={"tensor": t, "context": peer},
                device_id_type=MESH,
            ).start()

        return send

    def exchange(src, dst, sem):
        send = sender(src, dst, sem)
        far_peers(send)
        near_peers(send)
        dst[me] = src[me]

    def wait_all(buf, sem):
        view = buf.at[pl.ds(0, PEERS - 1)]
        pltpu.make_async_copy(view, view, sem).wait()

    early = ((sseq, rseq, 0), (sfilt.at[0], rfilt.at[0], 1))
    for src, dst, sem in early:
        near_peers(sender(src, dst, sem))
        dst[me] = src[me]
    pl.semaphore_wait(far_sem, 2)
    for src, dst, sem in early:
        far_peers(sender(src, dst, sem))
    exchange(sfilt.at[1], rfilt.at[1], 2)

    for load in loads[2:]:
        load.wait()
    eye = lax.broadcasted_iota(jnp.int32, (LOCAL_CH, LOCAL_CH), 0) == lax.broadcasted_iota(
        jnp.int32, (LOCAL_CH, LOCAL_CH), 1
    )
    skip_col = jnp.sum(jnp.where(eye, skip[...], 0.0), axis=1, keepdims=True)
    for s in range(SEQS):
        rows = pl.ds(s * LOCAL_CH, LOCAL_CH)
        for bh in range(4):
            skipped[bh, rows, :] = skip_col * seq32[bh, rows, :]
            gate32[bh, rows, :] = gate[s, :, pl.ds(bh * 128, 128)].astype(F32)
    for half in range(2):
        lanes = pl.ds(half * 128, 128)
        w32[half] = w_rows[:, lanes].astype(F32)
        for tt in range(RING * RING):
            for chl in range(2):
                rows = w32[half, pl.ds(tt * LOCAL_CH + chl, PEERS, stride=2), :].astype(BF16)
                wg[y, tt, chl, :, lanes] = rows
    w_copies = [
        pltpu.make_async_remote_copy(
            src_ref=wg.at[y],
            dst_ref=wg.at[y],
            send_sem=w_send.at[k - 1],
            recv_sem=w_recv.at[k - 1],
            device_id={"tensor": ring + (y + k) % RING, "context": me},
            device_id_type=MESH,
        )
        for k in range(1, RING)
    ]
    for c in w_copies:
        c.start()

    wait_all(rseq, a2a_recv.at[0])
    msg32[...] = rseq[...].reshape(PEERS * 16, 128).astype(F32)

    def base(chl, part, s):
        return ((chl * 2 + part) * 2 + s) * RES

    for chl in range(2):
        for s in range(SEQS):
            row = (s * 2 + chl) * 4
            tokens = jnp.concatenate(
                [msg32[pl.ds(row + bh, PEERS, stride=16), :] for bh in range(4)], axis=1
            ).astype(BF16)
            freq = dot(first[...], jnp.concatenate([tokens, tokens], axis=0))
            re, im = freq[:RES], freq[RES:]
            for part, value in enumerate((re * tw[0] + im * tw[1], im * tw[0] - re * tw[1])):
                hi, lo = split(value)
                lhs_hi[pl.ds(base(chl, part, s), RES), :] = hi
                lhs_lo[pl.ds(base(chl, part, s), RES), :] = lo

    def inner(which, rows):
        hi, lo = lhs_hi[rows, :], lhs_lo[rows, :]
        return dot(hi, dft[2 * which]) + dot(lo, dft[2 * which]) + dot(hi, dft[2 * which + 1])

    everything = pl.ds(0, 8 * RES)
    wide[0] = inner(0, everything)
    wide[1] = inner(1, everything)

    for chl in range(2):
        wait_all(rfilt.at[chl], a2a_recv.at[1 + chl])
        msg32[...] = rfilt[chl].reshape(PEERS * 16, 128).astype(F32)
        for ri in range(2):
            for j in range(2):
                for mh in range(4):
                    spec[ri, pl.ds(j * PEERS, PEERS), pl.ds(mh * 128, 128)] = msg32[
                        pl.ds(ri * 8 + mh * 2 + j, PEERS, stride=16), :
                    ]
        for s in range(SEQS):
            rows, rows_im = pl.ds(base(chl, 0, s), RES), pl.ds(base(chl, 1, s), RES)
            f_re = wide[0, rows, :] + wide[1, rows_im, :]
            f_im = wide[0, rows_im, :] - wide[1, rows, :]
            for which, value in (
                (rows, f_re * spec[0] - f_im * spec[1]),
                (rows_im, f_re * spec[1] + f_im * spec[0]),
            ):
                hi, lo = split(value)
                lhs_hi[which, :] = hi
                lhs_lo[which, :] = lo
        channel = pl.ds(chl * 4 * RES, 4 * RES)
        wide[0, channel, :] = inner(0, channel)
        wide[1, channel, :] = inner(1, channel)
        for s in range(SEQS):
            rows, rows_im = pl.ds(base(chl, 0, s), RES), pl.ds(base(chl, 1, s), RES)
            b_re = wide[0, rows, :] - wide[1, rows_im, :]
            b_im = wide[0, rows_im, :] + wide[1, rows, :]
            re_hi, re_lo = split(b_re * tw[0] - b_im * tw[1])
            im_hi, im_lo = split(b_im * tw[0] + b_re * tw[1])
            signal = dot(
                last[...], jnp.concatenate([re_hi, im_hi, re_lo, im_lo, re_hi, im_hi], axis=0)
            )
            for bh in range(4):
                msg32[pl.ds(s * 4 + bh, PEERS, stride=8), :] = signal[:, bh * 128 : (bh + 1) * 128]
        bsend[chl] = msg32[pl.ds(0, PEERS * 8), :].reshape(PEERS, 8, 128).astype(BF16)
        exchange(bsend.at[chl], brecv.at[chl], 3 + chl)

    def quarter_copy(chl, k):
        return pltpu.make_async_remote_copy(
            src_ref=mbuf.at[chl, (y + k) % RING],
            dst_ref=gbuf.at[zl, chl, y],
            send_sem=y_send.at[chl, k - 1],
            recv_sem=y_recv.at[chl],
            device_id={"tensor": ring + (y + k) % RING, "context": me},
            device_id_type=MESH,
        )

    def mix(chl):
        wait_all(brecv.at[chl], a2a_recv.at[3 + chl])
        msg32[pl.ds(0, PEERS * 8), :] = brecv[chl].astype(F32).reshape(PEERS * 8, 128)
        for bh in range(4):
            pieces = []
            for s in range(SEQS):
                rows = pl.ds(s * LOCAL_CH + chl, PEERS, stride=2)
                conv = msg32[pl.ds(s * 4 + bh, PEERS, stride=8), :]
                pieces.append(gate32[bh, rows, :] * (conv + skipped[bh, rows, :]))
            for s in range(SEQS):
                mbuf[chl, bh, s] = pieces[s].astype(BF16)
        for k in range(1, RING):
            quarter_copy(chl, k).start()
        gbuf[zl, chl, y] = mbuf[chl, y]

    def z_copy(origin, part, slot, target):
        ref = gbuf.at[origin, 0] if part == 0 else gbuf.at[origin, 1, :, part - 1]
        return pltpu.make_async_remote_copy(
            src_ref=ref,
            dst_ref=ref,
            send_sem=z_send.at[part, slot],
            recv_sem=z_recv.at[part, origin],
            device_id={"tensor": target, "context": me},
            device_id_type=MESH,
        )

    inner_chip = (zl == 1) | (zl == 2)
    partner = (zl + 1 - 2 * (zl % 2), (zl + 2) % RING, RING - 1 - zl)

    def z_sends(part, visit):
        for k in (2, 1):

            @pl.when(zl < RING - k)
            def _():
                visit(z_copy(zl, part, 2 * k - 2, t + k * RING))

            @pl.when(zl >= k)
            def _():
                visit(z_copy(zl, part, 2 * k - 1, t - k * RING))

    def pass_on(part):
        return z_copy(partner[1], part, 4, t + (2 * zl - 3) * RING)

    def wait_quarters(chl):
        view = gbuf.at[0, chl, pl.ds(0, RING - 1)]
        pltpu.make_async_copy(view, view, y_recv.at[chl]).wait()

    def z_wait(part, k):
        z_copy(partner[k - 1], part, 0, t).wait_recv()
        if k == 2:

            @pl.when(inner_chip)
            def _():
                pass_on(part).start()

    def tokens_of(z, chl, s):
        return gbuf[z, chl, :, s].astype(F32).reshape(128, 128).T.astype(BF16)

    def weights_of(z, chl, column):
        return jnp.concatenate([wg[column, z * RING + yy, chl] for yy in range(RING)], axis=0)

    def project(chl, s, items):
        lhs = jnp.concatenate([tokens_of(z, chl, s) for z in items], axis=1)

        def columns(column):
            return dot(lhs, jnp.concatenate([weights_of(z, chl, column) for z in items], axis=0))

        return columns

    def result_copy(s, k):
        column = (y + k) % RING
        return pltpu.make_async_remote_copy(
            src_ref=osend.at[s, column],
            dst_ref=out_ref.at[s, pl.ds(y * 128, 128), :],
            send_sem=o_send.at[s, k - 1],
            recv_sem=o_recv.at[s, k - 1],
            device_id={"tensor": ring + column, "context": me},
            device_id_type=MESH,
        )

    def own_result(s):
        return pltpu.make_async_copy(
            osend.at[s, y], out_ref.at[s, pl.ds(y * 128, 128), :], o_own.at[s]
        )

    mix(0)
    wait_quarters(0)
    z_sends(0, lambda c: c.start())
    mix(1)
    wait_quarters(1)
    for s in range(SEQS):
        z_sends(1 + s, lambda c: c.start())
    z_wait(0, 2)
    z_wait(0, 1)
    for c in w_copies:
        c.wait_recv()
    for s in range(SEQS):
        near = project(0, s, (zl, partner[0]))
        for column in range(RING):
            acc[s, column] = near(column)
    z_wait(1, 2)
    z_wait(0, 3)
    for s in range(SEQS):
        far = project(0, s, (partner[1], partner[2]))
        for column in range(RING):
            acc[s, column] += far(column)
    z_wait(2, 2)
    for s in range(SEQS):
        z_wait(1 + s, 1)
        near = project(1, s, (zl, partner[0]))
        for column in range(RING):
            acc[s, column] += near(column)
        z_wait(1 + s, 3)
        far = project(1, s, (partner[1], partner[2]))
        for k in (2, 1, 3, 0):
            column = (y + k) % RING
            osend[s, column] = (acc[s, column] + far(column)).astype(BF16)
            if k:
                result_copy(s, k).start()
            else:
                own_result(s).start()
    for s in range(SEQS):
        own_result(s).wait()
        for k in range(1, RING):
            result_copy(s, k).wait_recv()

    for part in range(3):
        z_sends(part, lambda c: c.wait_send())

        @pl.when(inner_chip)
        def _():
            pass_on(part).wait_send()

    for k in range(1, RING):
        w_copies[k - 1].wait_send()
        for s in range(SEQS):
            result_copy(s, k).wait_send()
        for chl in range(2):
            quarter_copy(chl, k).wait_send()
    for i, buf in enumerate((sseq, sfilt.at[0], sfilt.at[1], bsend.at[0], bsend.at[1])):
        wait_all(buf, a2a_send.at[i])


def local(sequence, gate, skip, filter_spectrum, out_weight):
    first, last, dft, twiddle = tables()
    rows = filter_spectrum.reshape(2, LOCAL_CH, 2, 4, 128).transpose(0, 1, 3, 2, 4).reshape(-1, 128)
    hbm = pl.BlockSpec(memory_space=pl.ANY)
    return pl.pallas_call(
        kernel,
        out_shape=jax.ShapeDtypeStruct((SEQS, BLOCK, COLS), BF16),
        in_specs=[hbm] * 9,
        out_specs=hbm,
        scratch_shapes=[
            pltpu.VMEM((SEQS, LOCAL_CH, BLOCK), BF16),
            pltpu.VMEM((PEERS * 32, 128), F32),
            pltpu.VMEM((1, LOCAL_CH), F32),
            pltpu.VMEM((2 * RES, 2 * PEERS), BF16),
            pltpu.VMEM((PEERS, 6 * RES), BF16),
            pltpu.VMEM((SEQS, LOCAL_CH, BLOCK), BF16),
            pltpu.VMEM((RING * RING * LOCAL_CH, COLS), BF16),
            pltpu.VMEM((4, BLOCK, BLOCK), BF16),
            pltpu.VMEM((2, RES, BLOCK), F32),
            pltpu.VMEM((4, SEQS * LOCAL_CH, 128), F32),
            pltpu.VMEM((4, SEQS * LOCAL_CH, 128), F32),
            pltpu.VMEM((4, SEQS * LOCAL_CH, 128), F32),
            pltpu.VMEM((2, RING * RING * LOCAL_CH, 128), F32),
            pltpu.VMEM((PEERS * 16, 128), F32),
            pltpu.VMEM((PEERS, 16, 128), BF16),
            pltpu.VMEM((PEERS, 16, 128), BF16),
            pltpu.VMEM((2, PEERS, 16, 128), BF16),
            pltpu.VMEM((2, PEERS, 16, 128), BF16),
            pltpu.VMEM((2, RES, BLOCK), F32),
            pltpu.VMEM((2, 8 * RES, BLOCK), F32),
            pltpu.VMEM((8 * RES, BLOCK), BF16),
            pltpu.VMEM((8 * RES, BLOCK), BF16),
            pltpu.VMEM((2, PEERS, 8, 128), BF16),
            pltpu.VMEM((2, PEERS, 8, 128), BF16),
            pltpu.VMEM((2, RING, SEQS, PEERS, 128), BF16),
            pltpu.VMEM((RING, 2, RING, SEQS, PEERS, 128), BF16),
            pltpu.VMEM((RING, RING * RING, 2, PEERS, COLS), BF16),
            pltpu.VMEM((SEQS, RING, 128, COLS), F32),
            pltpu.VMEM((SEQS, RING, 128, COLS), BF16),
            pltpu.SemaphoreType.DMA((9,)),
            pltpu.SemaphoreType.DMA((5,)),
            pltpu.SemaphoreType.DMA((5,)),
            pltpu.SemaphoreType.DMA((RING - 1,)),
            pltpu.SemaphoreType.DMA((RING - 1,)),
            pltpu.SemaphoreType.DMA((2, RING - 1)),
            pltpu.SemaphoreType.DMA((2,)),
            pltpu.SemaphoreType.DMA((3, 5)),
            pltpu.SemaphoreType.DMA((3, RING)),
            pltpu.SemaphoreType.DMA((SEQS, RING - 1)),
            pltpu.SemaphoreType.DMA((SEQS, RING - 1)),
            pltpu.SemaphoreType.DMA((SEQS,)),
            pltpu.SemaphoreType.REGULAR,
        ],
        compiler_params=pltpu.CompilerParams(
            collective_id=0, has_side_effects=True, vmem_limit_bytes=62 * 1024 * 1024
        ),
    )(
        sequence, rows, skip.reshape(1, LOCAL_CH), jnp.asarray(first), jnp.asarray(last),
        gate, out_weight, jnp.asarray(dft), jnp.asarray(twiddle),
    )


def solution(mesh):
    in_specs = (
        P(None, "tensor", "context"),
        P(None, "tensor", "context"),
        P("tensor"),
        P(None, "tensor", "context", None),
        P(None, "tensor"),
    )
    out_specs = P(None, "context", "tensor")
    return jax.shard_map(local, mesh=mesh, in_specs=in_specs, out_specs=out_specs, check_vma=False)
```

```python
import functools
import math

import jax
import jax.numpy as jnp
import ml_dtypes
import numpy as np
from jax import lax
from jax.experimental import pallas as pl
from jax.experimental.pallas import tpu as pltpu
from jax.sharding import PartitionSpec as P

MESH = pl.DeviceIdType.MESH
BF16 = jnp.bfloat16
F32 = jnp.float32

SEQS = 2
PEERS = 32
RING = 4
LOCAL_CH = 64
BLOCK = 512
RES = 64
COLS = 256
FFT = RES * BLOCK


def split_hi_lo(table):
    hi = table.astype(ml_dtypes.bfloat16)
    lo = (table - hi.astype(np.float64)).astype(ml_dtypes.bfloat16)
    return hi, lo


@functools.lru_cache(maxsize=None)
def tables():
    row = np.arange(RES)
    residue = 2 * (row % PEERS) + row // PEERS
    source = np.arange(PEERS)
    pos = np.arange(BLOCK)
    outer = 2.0 * math.pi * (residue[:, None] * source[None, :] % RES) / RES
    first = np.concatenate([np.cos(outer), -np.sin(outer)], axis=0)
    first = np.concatenate(split_hi_lo(first), axis=1)
    last = np.concatenate([np.cos(outer).T, -np.sin(outer).T], axis=1) / FFT
    last_hi, last_lo = split_hi_lo(last)
    last = np.concatenate([last_hi, last_hi, last_lo], axis=1)
    inner = 2.0 * math.pi * (pos[:, None] * pos[None, :] % BLOCK) / BLOCK
    dft = np.stack([*split_hi_lo(np.cos(inner)), *split_hi_lo(np.sin(inner))])
    turn = 2.0 * math.pi * (residue[:, None] * pos[None, :] % FFT) / FFT
    twiddle = np.stack([np.cos(turn), np.sin(turn)]).astype(np.float32)
    return first, last, dft, twiddle


def dot(a, b):
    return jnp.dot(a, b, preferred_element_type=F32)


def split(value):
    hi = value.astype(BF16)
    return hi, (value - hi.astype(F32)).astype(BF16)


def kernel(
    seq_hbm, filt_hbm, skip_hbm, first_hbm, last_hbm, gate_hbm, w_hbm, dft_hbm, tw_hbm,
    out_ref,
    seq, filt, skip, first, last, gate, w_rows, dft, tw,
    seq32, gate32, skipped, w32, msg32, sseq, rseq, sfilt, rfilt, spec, wide, lhs_hi, lhs_lo,
    bsend, brecv, mbuf, gbuf, wg, acc, osend,
    load_sem, a2a_send, a2a_recv, w_send, w_recv, y_send, y_recv, z_send, z_recv, o_send, o_recv, o_own, far_sem,
):
    me = lax.axis_index("context")
    t = lax.axis_index("tensor")
    x, zh, core = me // 8, (me // 2) % 4, me % 2
    zl, y = t // RING, t % RING
    ring = zl * RING

    def peers(lo, hi, visit):
        def step(j, carry):
            steps = jnp.where(j < 8, 2, jnp.where(j < 16, 1, jnp.where(j < 24, 3, 0)))
            visit(
                ((x + 2 + (j // 2) % 4) % 4) * 8 + ((zh + steps) % 4) * 2 + (core + j) % 2
            )
            return carry

        lax.fori_loop(lo, hi, step, 0)

    def near_peers(visit):
        peers(8, 28, visit)
        peers(29, PEERS, visit)

    def far_peers(visit):
        peers(0, 8, visit)

    loads = [
        pltpu.make_async_copy(src, dst, load_sem.at[i])
        for i, (src, dst) in enumerate(
            [
                (seq_hbm, seq), (filt_hbm, filt), (skip_hbm, skip), (first_hbm, first),
                (last_hbm, last), (gate_hbm, gate), (w_hbm, w_rows), (tw_hbm, tw), (dft_hbm, dft),
            ]
        )
    ]
    for load in loads[:2]:
        load.start()

    barrier = pltpu.get_barrier_semaphore()

    def greet(tensor, context):
        pl.semaphore_signal(
            barrier, inc=1, device_id={"tensor": tensor, "context": context}, device_id_type=MESH
        )

    near_peers(lambda peer: greet(t, peer))
    for k in range(1, RING):
        greet(ring + (y + k) % RING, me)
    for k in (1, 2):

        @pl.when(zl < RING - k)
        def _():
            greet(t + k * RING, me)

        @pl.when(zl >= k)
        def _():
            greet(t - k * RING, me)

    for load in loads[2:]:
        load.start()

    loads[0].wait()
    for s in range(SEQS):
        for bh in range(4):
            seq32[bh, pl.ds(s * LOCAL_CH, LOCAL_CH), :] = seq[s, :, pl.ds(bh * 128, 128)].astype(F32)
    for s in range(SEQS):
        for chl in range(2):
            for bh in range(4):
                msg32[pl.ds((s * 2 + chl) * 4 + bh, PEERS, stride=16), :] = seq32[
                    bh, pl.ds(s * LOCAL_CH + chl, PEERS, stride=2), :
                ]
    sseq[...] = msg32[...].reshape(PEERS, 16, 128).astype(BF16)
    z_neighbours = jnp.where((zl == 0) | (zl == RING - 1), 2, 3)
    pl.semaphore_wait(barrier, 23 + 3 + z_neighbours)
    next_up, next_down = (
        x * 8 + ((zh + 1) % 4) * 2 + core,
        x * 8 + ((zh + 3) % 4) * 2 + core,
    )
    for peer in (next_up, next_down):
        pl.semaphore_signal(
            far_sem, inc=1, device_id={"tensor": t, "context": peer}, device_id_type=MESH
        )

    def sender(src, dst, sem):
        def send(peer):
            pltpu.make_async_remote_copy(
                src_ref=src.at[peer],
                dst_ref=dst.at[me],
                send_sem=a2a_send.at[sem],
                recv_sem=a2a_recv.at[sem],
                device_id={"tensor": t, "context": peer},
                device_id_type=MESH,
            ).start()

        return send

    def exchange(src, dst, sem):
        send = sender(src, dst, sem)
        far_peers(send)
        near_peers(send)
        dst[me] = src[me]

    def wait_all(buf, sem):
        view = buf.at[pl.ds(0, PEERS - 1)]
        pltpu.make_async_copy(view, view, sem).wait()

    near_peers(sender(sseq, rseq, 0))
    rseq[me] = sseq[me]
    loads[1].wait()
    parts = filt[...].reshape(2, PEERS, 2, 8, 128)
    for chl in range(2):
        sfilt[chl] = jnp.concatenate([parts[0, :, chl], parts[1, :, chl]], axis=1).astype(BF16)
    early = ((sseq, rseq, 0), (sfilt.at[0], rfilt.at[0], 1))
    near_peers(sender(*early[1]))
    rfilt[0, me] = sfilt[0, me]
    pl.semaphore_wait(far_sem, 2)
    for src, dst, sem in early:
        far_peers(sender(src, dst, sem))
    exchange(sfilt.at[1], rfilt.at[1], 2)

    for load in loads[2:]:
        load.wait()
    eye = lax.broadcasted_iota(jnp.int32, (LOCAL_CH, LOCAL_CH), 0) == lax.broadcasted_iota(
        jnp.int32, (LOCAL_CH, LOCAL_CH), 1
    )
    skip_col = jnp.sum(jnp.where(eye, skip[...], 0.0), axis=1, keepdims=True)
    for s in range(SEQS):
        rows = pl.ds(s * LOCAL_CH, LOCAL_CH)
        for bh in range(4):
            skipped[bh, rows, :] = skip_col * seq32[bh, rows, :]
            gate32[bh, rows, :] = gate[s, :, pl.ds(bh * 128, 128)].astype(F32)
    for half in range(2):
        lanes = pl.ds(half * 128, 128)
        w32[half] = w_rows[:, lanes].astype(F32)
        for tt in range(RING * RING):
            for chl in range(2):
                rows = w32[half, pl.ds(tt * LOCAL_CH + chl, PEERS, stride=2), :].astype(BF16)
                wg[y, tt, chl, :, lanes] = rows
    w_copies = [
        pltpu.make_async_remote_copy(
            src_ref=wg.at[y],
            dst_ref=wg.at[y],
            send_sem=w_send.at[k - 1],
            recv_sem=w_recv.at[k - 1],
            device_id={"tensor": ring + (y + k) % RING, "context": me},
            device_id_type=MESH,
        )
        for k in range(1, RING)
    ]
    for c in w_copies:
        c.start()

    wait_all(rseq, a2a_recv.at[0])
    msg32[...] = rseq[...].reshape(PEERS * 16, 128).astype(F32)

    def base(chl, part, s):
        return ((chl * 2 + part) * 2 + s) * RES

    for chl in range(2):
        for s in range(SEQS):
            row = (s * 2 + chl) * 4
            tokens = jnp.concatenate(
                [msg32[pl.ds(row + bh, PEERS, stride=16), :] for bh in range(4)], axis=1
            ).astype(BF16)
            freq = dot(first[...], jnp.concatenate([tokens, tokens], axis=0))
            re, im = freq[:RES], freq[RES:]
            for part, value in enumerate((re * tw[0] + im * tw[1], im * tw[0] - re * tw[1])):
                hi, lo = split(value)
                lhs_hi[pl.ds(base(chl, part, s), RES), :] = hi
                lhs_lo[pl.ds(base(chl, part, s), RES), :] = lo

    def inner(which, rows):
        hi = lhs_hi[rows, :]
        return dot(hi, dft[2 * which]) + dot(hi, dft[2 * which + 1])

    for chl in range(2):
        channel = pl.ds(chl * 4 * RES, 4 * RES)
        for which in range(2):
            wide[which] = inner(which, channel) + dot(lhs_lo[channel, :], dft[2 * which])
        wait_all(rfilt.at[chl], a2a_recv.at[1 + chl])
        msg32[...] = rfilt[chl].reshape(PEERS * 16, 128).astype(F32)
        for ri in range(2):
            for j in range(2):
                for mh in range(4):
                    spec[ri, pl.ds(j * PEERS, PEERS), pl.ds(mh * 128, 128)] = msg32[
                        pl.ds(ri * 8 + mh * 2 + j, PEERS, stride=16), :
                    ]
        for s in range(SEQS):
            rows, rows_im = pl.ds(s * RES, RES), pl.ds((2 + s) * RES, RES)
            f_re = wide[0, rows, :] + wide[1, rows_im, :]
            f_im = wide[0, rows_im, :] - wide[1, rows, :]
            lhs_hi[pl.ds(base(chl, 0, s), RES), :] = (f_re * spec[0] - f_im * spec[1]).astype(BF16)
            lhs_hi[pl.ds(base(chl, 1, s), RES), :] = (f_re * spec[1] + f_im * spec[0]).astype(BF16)
        for which in range(2):
            wide[which] = inner(which, channel)
        for s in range(SEQS):
            rows, rows_im = pl.ds(s * RES, RES), pl.ds((2 + s) * RES, RES)
            b_re = wide[0, rows, :] - wide[1, rows_im, :]
            b_im = wide[0, rows_im, :] + wide[1, rows, :]
            re_hi, re_lo = split(b_re * tw[0] - b_im * tw[1])
            im_hi, im_lo = split(b_im * tw[0] + b_re * tw[1])
            signal = dot(
                last[...], jnp.concatenate([re_hi, im_hi, re_lo, im_lo, re_hi, im_hi], axis=0)
            )
            for bh in range(4):
                msg32[pl.ds(s * 4 + bh, PEERS, stride=8), :] = signal[:, bh * 128 : (bh + 1) * 128]
        bsend[chl] = msg32[pl.ds(0, PEERS * 8), :].reshape(PEERS, 8, 128).astype(BF16)
        exchange(bsend.at[chl], brecv.at[chl], 3 + chl)

    def quarter_copy(chl, k):
        return pltpu.make_async_remote_copy(
            src_ref=mbuf.at[chl, (y + k) % RING],
            dst_ref=gbuf.at[zl, chl, RING - k],
            send_sem=y_send.at[chl, k - 1],
            recv_sem=y_recv.at[chl],
            device_id={"tensor": ring + (y + k) % RING, "context": me},
            device_id_type=MESH,
        )

    def mix(chl):
        wait_all(brecv.at[chl], a2a_recv.at[3 + chl])
        msg32[pl.ds(0, PEERS * 8), :] = brecv[chl].astype(F32).reshape(PEERS * 8, 128)
        for bh in range(4):
            pieces = []
            for s in range(SEQS):
                rows = pl.ds(s * LOCAL_CH + chl, PEERS, stride=2)
                conv = msg32[pl.ds(s * 4 + bh, PEERS, stride=8), :]
                pieces.append(gate32[bh, rows, :] * (conv + skipped[bh, rows, :]))
            for s in range(SEQS):
                mbuf[chl, bh, s] = pieces[s].astype(BF16)
        for k in (2, 1, 3):
            quarter_copy(chl, k).start()
        gbuf[zl, chl, 0] = mbuf[chl, y]

    def z_copy(origin, part, slot, target):
        others = pl.ds(1, RING - 1)
        ref = (
            gbuf.at[origin, 0, 0],
            gbuf.at[origin, 0, others],
            gbuf.at[origin, 1, 0],
            gbuf.at[origin, 1, others, 0],
            gbuf.at[origin, 1, others, 1],
        )[part]
        return pltpu.make_async_remote_copy(
            src_ref=ref,
            dst_ref=ref,
            send_sem=z_send.at[part, slot],
            recv_sem=z_recv.at[part, origin],
            device_id={"tensor": target, "context": me},
            device_id_type=MESH,
        )

    inner_chip = (zl == 1) | (zl == 2)
    partner = (zl + 1 - 2 * (zl % 2), (zl + 2) % RING, RING - 1 - zl)

    def z_sends(part, visit):
        for k in (2, 1):

            @pl.when(zl < RING - k)
            def _():
                visit(z_copy(zl, part, 2 * k - 2, t + k * RING))

            @pl.when(zl >= k)
            def _():
                visit(z_copy(zl, part, 2 * k - 1, t - k * RING))

    def pass_on(part):
        return z_copy(partner[1], part, 4, t + (2 * zl - 3) * RING)

    def wait_quarters(chl):
        view = gbuf.at[0, chl, pl.ds(0, RING - 1)]
        pltpu.make_async_copy(view, view, y_recv.at[chl]).wait()

    def z_wait(part, k):
        z_copy(partner[k - 1], part, 0, t).wait_recv()
        if k == 2:

            @pl.when(inner_chip)
            def _():
                pass_on(part).start()

    def tokens_of(z, chl, s):
        return gbuf[z, chl, :, s].astype(F32).reshape(128, 128).T.astype(BF16)

    def weights_of(z, chl, column):
        return jnp.concatenate(
            [wg[column, z * RING + (y + r) % RING, chl] for r in range(RING)], axis=0
        )

    def project(chl, s, items):
        lhs = jnp.concatenate([tokens_of(z, chl, s) for z in items], axis=1)

        def columns(column):
            return dot(lhs, jnp.concatenate([weights_of(z, chl, column) for z in items], axis=0))

        return columns

    def result_copy(s, k):
        column = (y + k) % RING
        return pltpu.make_async_remote_copy(
            src_ref=osend.at[s, column],
            dst_ref=out_ref.at[s, pl.ds(y * 128, 128), :],
            send_sem=o_send.at[s, k - 1],
            recv_sem=o_recv.at[s, k - 1],
            device_id={"tensor": ring + column, "context": me},
            device_id_type=MESH,
        )

    def own_result(s):
        return pltpu.make_async_copy(
            osend.at[s, y], out_ref.at[s, pl.ds(y * 128, 128), :], o_own.at[s]
        )

    def start(part):
        z_sends(part, lambda c: c.start())

    mix(0)
    start(0)
    wait_quarters(0)
    start(1)
    mix(1)
    start(2)
    z_wait(0, 2)
    wait_quarters(1)
    start(3)
    start(4)
    z_wait(1, 2)
    z_wait(2, 2)
    z_wait(0, 1)
    z_wait(1, 1)
    for c in w_copies:
        c.wait_recv()
    for s in range(SEQS):
        near = project(0, s, (zl, partner[0]))
        for column in range(RING):
            acc[s, column] = near(column)
    z_wait(3, 2)
    z_wait(0, 3)
    z_wait(1, 3)
    for s in range(SEQS):
        far = project(0, s, (partner[1], partner[2]))
        for column in range(RING):
            acc[s, column] += far(column)
    z_wait(4, 2)
    z_wait(2, 1)
    z_wait(2, 3)
    for s in range(SEQS):
        z_wait(3 + s, 1)
        near = project(1, s, (zl, partner[0]))
        for column in range(RING):
            acc[s, column] += near(column)
        z_wait(3 + s, 3)
        far = project(1, s, (partner[1], partner[2]))
        for k in (2, 1, 3, 0):
            column = (y + k) % RING
            osend[s, column] = (acc[s, column] + far(column)).astype(BF16)
            if k:
                result_copy(s, k).start()
            else:
                own_result(s).start()
    for s in range(SEQS):
        own_result(s).wait()
        for k in range(1, RING):
            result_copy(s, k).wait_recv()

    for part in range(5):
        z_sends(part, lambda c: c.wait_send())

        @pl.when(inner_chip)
        def _():
            pass_on(part).wait_send()

    for k in range(1, RING):
        w_copies[k - 1].wait_send()
        for s in range(SEQS):
            result_copy(s, k).wait_send()
        for chl in range(2):
            quarter_copy(chl, k).wait_send()
    for i, buf in enumerate((sseq, sfilt.at[0], sfilt.at[1], bsend.at[0], bsend.at[1])):
        wait_all(buf, a2a_send.at[i])


def local(sequence, gate, skip, filter_spectrum, out_weight):
    first, last, dft, twiddle = tables()
    rows = filter_spectrum.reshape(2, LOCAL_CH, 2, 4, 128).transpose(0, 1, 3, 2, 4).reshape(-1, 128)
    hbm = pl.BlockSpec(memory_space=pl.ANY)
    return pl.pallas_call(
        kernel,
        out_shape=jax.ShapeDtypeStruct((SEQS, BLOCK, COLS), BF16),
        in_specs=[hbm] * 9,
        out_specs=hbm,
        scratch_shapes=[
            pltpu.VMEM((SEQS, LOCAL_CH, BLOCK), BF16),
            pltpu.VMEM((PEERS * 32, 128), F32),
            pltpu.VMEM((1, LOCAL_CH), F32),
            pltpu.VMEM((2 * RES, 2 * PEERS), BF16),
            pltpu.VMEM((PEERS, 6 * RES), BF16),
            pltpu.VMEM((SEQS, LOCAL_CH, BLOCK), BF16),
            pltpu.VMEM((RING * RING * LOCAL_CH, COLS), BF16),
            pltpu.VMEM((4, BLOCK, BLOCK), BF16),
            pltpu.VMEM((2, RES, BLOCK), F32),
            pltpu.VMEM((4, SEQS * LOCAL_CH, 128), F32),
            pltpu.VMEM((4, SEQS * LOCAL_CH, 128), F32),
            pltpu.VMEM((4, SEQS * LOCAL_CH, 128), F32),
            pltpu.VMEM((2, RING * RING * LOCAL_CH, 128), F32),
            pltpu.VMEM((PEERS * 16, 128), F32),
            pltpu.VMEM((PEERS, 16, 128), BF16),
            pltpu.VMEM((PEERS, 16, 128), BF16),
            pltpu.VMEM((2, PEERS, 16, 128), BF16),
            pltpu.VMEM((2, PEERS, 16, 128), BF16),
            pltpu.VMEM((2, RES, BLOCK), F32),
            pltpu.VMEM((2, 4 * RES, BLOCK), F32),
            pltpu.VMEM((8 * RES, BLOCK), BF16),
            pltpu.VMEM((8 * RES, BLOCK), BF16),
            pltpu.VMEM((2, PEERS, 8, 128), BF16),
            pltpu.VMEM((2, PEERS, 8, 128), BF16),
            pltpu.VMEM((2, RING, SEQS, PEERS, 128), BF16),
            pltpu.VMEM((RING, 2, RING, SEQS, PEERS, 128), BF16),
            pltpu.VMEM((RING, RING * RING, 2, PEERS, COLS), BF16),
            pltpu.VMEM((SEQS, RING, 128, COLS), F32),
            pltpu.VMEM((SEQS, RING, 128, COLS), BF16),
            pltpu.SemaphoreType.DMA((9,)),
            pltpu.SemaphoreType.DMA((5,)),
            pltpu.SemaphoreType.DMA((5,)),
            pltpu.SemaphoreType.DMA((RING - 1,)),
            pltpu.SemaphoreType.DMA((RING - 1,)),
            pltpu.SemaphoreType.DMA((2, RING - 1)),
            pltpu.SemaphoreType.DMA((2,)),
            pltpu.SemaphoreType.DMA((5, 5)),
            pltpu.SemaphoreType.DMA((5, RING)),
            pltpu.SemaphoreType.DMA((SEQS, RING - 1)),
            pltpu.SemaphoreType.DMA((SEQS, RING - 1)),
            pltpu.SemaphoreType.DMA((SEQS,)),
            pltpu.SemaphoreType.REGULAR,
        ],
        compiler_params=pltpu.CompilerParams(
            collective_id=0, has_side_effects=True, vmem_limit_bytes=62 * 1024 * 1024
        ),
    )(
        sequence, rows, skip.reshape(1, LOCAL_CH), jnp.asarray(first), jnp.asarray(last),
        gate, out_weight, jnp.asarray(dft), jnp.asarray(twiddle),
    )


def solution(mesh):
    in_specs = (
        P(None, "tensor", "context"),
        P(None, "tensor", "context"),
        P("tensor"),
        P(None, "tensor", "context", None),
        P(None, "tensor"),
    )
    out_specs = P(None, "context", "tensor")
    return jax.shard_map(local, mesh=mesh, in_specs=in_specs, out_specs=out_specs, check_vma=False)
```

```python
import functools
import math

import jax
import jax.numpy as jnp
import ml_dtypes
import numpy as np
from jax import lax
from jax.experimental import pallas as pl
from jax.experimental.pallas import tpu as pltpu
from jax.sharding import PartitionSpec as P

MESH = pl.DeviceIdType.MESH
BF16 = jnp.bfloat16
F32 = jnp.float32

SEQS = 2
PEERS = 32
RING = 4
LOCAL_CH = 64
BLOCK = 512
RES = 64
COLS = 256
FFT = RES * BLOCK


def split_hi_lo(table):
    hi = table.astype(ml_dtypes.bfloat16)
    lo = (table - hi.astype(np.float64)).astype(ml_dtypes.bfloat16)
    return hi, lo


@functools.lru_cache(maxsize=None)
def tables():
    row = np.arange(RES)
    residue = 2 * (row % PEERS) + row // PEERS
    source = np.arange(PEERS)
    pos = np.arange(BLOCK)
    outer = 2.0 * math.pi * (residue[:, None] * source[None, :] % RES) / RES
    first = np.concatenate([np.cos(outer), -np.sin(outer)], axis=0)
    first = np.concatenate(split_hi_lo(first), axis=1)
    last = np.concatenate([np.cos(outer).T, -np.sin(outer).T], axis=1) / FFT
    last_hi, last_lo = split_hi_lo(last)
    last = np.concatenate([last_hi, last_hi, last_lo], axis=1)
    inner = 2.0 * math.pi * (pos[:, None] * pos[None, :] % BLOCK) / BLOCK
    dft = np.stack([*split_hi_lo(np.cos(inner)), *split_hi_lo(np.sin(inner))])
    turn = 2.0 * math.pi * (residue[:, None] * pos[None, :] % FFT) / FFT
    twiddle = np.stack([np.cos(turn), np.sin(turn)]).astype(np.float32)
    return first, last, dft, twiddle


def dot(a, b):
    return jnp.dot(a, b, preferred_element_type=F32)


def split(value):
    hi = value.astype(BF16)
    return hi, (value - hi.astype(F32)).astype(BF16)


def kernel(
    seq_hbm, filt_hbm, skip_hbm, first_hbm, last_hbm, gate_hbm, w_hbm, dft_hbm, tw_hbm,
    out_ref,
    seq, filt, skip, first, last, gate, w_rows, dft, tw,
    seq32, gate32, skipped, w32, msg32, sseq, rseq, sfilt, rfilt, spec, wide, lhs_hi, lhs_lo,
    bsend, brecv, mbuf, gbuf, wg, acc, osend,
    load_sem, a2a_send, a2a_recv, w_send, w_recv, y_send, y_recv, z_send, z_recv, o_send, o_recv, o_own, far_sem,
):
    me = lax.axis_index("context")
    t = lax.axis_index("tensor")
    x, zh, core = me // 8, (me // 2) % 4, me % 2
    zl, y = t // RING, t % RING
    ring = zl * RING

    def peers(lo, hi, visit):
        def step(j, carry):
            steps = jnp.where(j < 8, 2, jnp.where(j < 16, 1, jnp.where(j < 24, 3, 0)))
            visit(
                ((x + 2 + (j // 2) % 4) % 4) * 8 + ((zh + steps) % 4) * 2 + (core + j) % 2
            )
            return carry

        lax.fori_loop(lo, hi, step, 0)

    def near_peers(visit):
        peers(8, 28, visit)
        peers(29, PEERS, visit)

    def far_peers(visit):
        peers(0, 8, visit)

    loads = [
        pltpu.make_async_copy(src, dst, load_sem.at[i])
        for i, (src, dst) in enumerate(
            [
                (seq_hbm, seq), (filt_hbm, filt), (skip_hbm, skip), (first_hbm, first),
                (last_hbm, last), (gate_hbm, gate), (w_hbm, w_rows), (tw_hbm, tw), (dft_hbm, dft),
            ]
        )
    ]
    for load in loads[:2]:
        load.start()

    barrier = pltpu.get_barrier_semaphore()

    def greet(tensor, context):
        pl.semaphore_signal(
            barrier, inc=1, device_id={"tensor": tensor, "context": context}, device_id_type=MESH
        )

    near_peers(lambda peer: greet(t, peer))
    for k in range(1, RING):
        greet(ring + (y + k) % RING, me)
    for k in (1, 2):

        @pl.when(zl < RING - k)
        def _():
            greet(t + k * RING, me)

        @pl.when(zl >= k)
        def _():
            greet(t - k * RING, me)

    for load in loads[2:]:
        load.start()

    loads[0].wait()
    for s in range(SEQS):
        for bh in range(4):
            seq32[bh, pl.ds(s * LOCAL_CH, LOCAL_CH), :] = seq[s, :, pl.ds(bh * 128, 128)].astype(F32)
    for s in range(SEQS):
        for chl in range(2):
            for bh in range(4):
                msg32[pl.ds((s * 2 + chl) * 4 + bh, PEERS, stride=16), :] = seq32[
                    bh, pl.ds(s * LOCAL_CH + chl, PEERS, stride=2), :
                ]
    sseq[...] = msg32[pl.ds(0, PEERS * 16), :].reshape(PEERS, 16, 128).astype(BF16)
    z_neighbours = jnp.where((zl == 0) | (zl == RING - 1), 2, 3)
    pl.semaphore_wait(barrier, 23 + 3 + z_neighbours)
    next_up, next_down = (
        x * 8 + ((zh + 1) % 4) * 2 + core,
        x * 8 + ((zh + 3) % 4) * 2 + core,
    )
    for peer in (next_up, next_down):
        pl.semaphore_signal(
            far_sem, inc=1, device_id={"tensor": t, "context": peer}, device_id_type=MESH
        )

    def sender(src, dst, sem):
        def send(peer):
            pltpu.make_async_remote_copy(
                src_ref=src.at[peer],
                dst_ref=dst.at[me],
                send_sem=a2a_send.at[sem],
                recv_sem=a2a_recv.at[sem],
                device_id={"tensor": t, "context": peer},
                device_id_type=MESH,
            ).start()

        return send

    def exchange(src, dst, sem):
        send = sender(src, dst, sem)
        far_peers(send)
        near_peers(send)
        dst[me] = src[me]

    def wait_all(buf, sem):
        view = buf.at[pl.ds(0, PEERS - 1)]
        pltpu.make_async_copy(view, view, sem).wait()

    near_peers(sender(sseq, rseq, 0))
    rseq[me] = sseq[me]
    loads[1].wait()
    parts = filt[...].reshape(2, PEERS, 2, 8, 128)
    for chl in range(2):
        sfilt[chl] = jnp.concatenate([parts[0, :, chl], parts[1, :, chl]], axis=1).astype(BF16)
    early = ((sseq, rseq, 0), (sfilt.at[0], rfilt.at[0], 1))
    near_peers(sender(*early[1]))
    rfilt[0, me] = sfilt[0, me]
    pl.semaphore_wait(far_sem, 2)
    for src, dst, sem in early:
        far_peers(sender(src, dst, sem))
    exchange(sfilt.at[1], rfilt.at[1], 2)

    for load in loads[2:]:
        load.wait()
    eye = lax.broadcasted_iota(jnp.int32, (LOCAL_CH, LOCAL_CH), 0) == lax.broadcasted_iota(
        jnp.int32, (LOCAL_CH, LOCAL_CH), 1
    )
    skip_col = jnp.sum(jnp.where(eye, skip[...], 0.0), axis=1, keepdims=True)
    for s in range(SEQS):
        rows = pl.ds(s * LOCAL_CH, LOCAL_CH)
        for bh in range(4):
            skipped[bh, rows, :] = skip_col * seq32[bh, rows, :]
            gate32[bh, rows, :] = gate[s, :, pl.ds(bh * 128, 128)].astype(F32)
    for half in range(2):
        lanes = pl.ds(half * 128, 128)
        w32[half, pl.ds(0, RING * RING * LOCAL_CH), :] = w_rows[:, lanes].astype(F32)
        for tt in range(RING * RING):
            for chl in range(2):
                rows = w32[half, pl.ds(tt * LOCAL_CH + chl, PEERS, stride=2), :].astype(BF16)
                wg[y, tt, chl, :, lanes] = rows
    w_copies = [
        pltpu.make_async_remote_copy(
            src_ref=wg.at[y],
            dst_ref=wg.at[y],
            send_sem=w_send.at[k - 1],
            recv_sem=w_recv.at[k - 1],
            device_id={"tensor": ring + (y + k) % RING, "context": me},
            device_id_type=MESH,
        )
        for k in range(1, RING)
    ]
    for c in w_copies:
        c.start()

    wait_all(rseq, a2a_recv.at[0])
    msg32[pl.ds(0, PEERS * 16), :] = rseq[...].reshape(PEERS * 16, 128).astype(F32)

    def base(chl, part, s):
        return ((chl * 2 + part) * 2 + s) * RES

    for chl in range(2):
        for s in range(SEQS):
            row = (s * 2 + chl) * 4
            tokens = jnp.concatenate(
                [msg32[pl.ds(row + bh, PEERS, stride=16), :] for bh in range(4)], axis=1
            ).astype(BF16)
            freq = dot(first[...], jnp.concatenate([tokens, tokens], axis=0))
            re, im = freq[:RES], freq[RES:]
            for part, value in enumerate((re * tw[0] + im * tw[1], im * tw[0] - re * tw[1])):
                hi, lo = split(value)
                lhs_hi[pl.ds(base(chl, part, s), RES), :] = hi
                lhs_lo[pl.ds(base(chl, part, s), RES), :] = lo

    def inner(which, rows):
        hi = lhs_hi[rows, :]
        return dot(hi, dft[2 * which]) + dot(hi, dft[2 * which + 1])

    for chl in range(2):
        channel = pl.ds(chl * 4 * RES, 4 * RES)
        for which in range(2):
            wide[which] = inner(which, channel) + dot(lhs_lo[channel, :], dft[2 * which])
        wait_all(rfilt.at[chl], a2a_recv.at[1 + chl])
        msg32[pl.ds(0, PEERS * 16), :] = rfilt[chl].reshape(PEERS * 16, 128).astype(F32)
        for ri in range(2):
            for j in range(2):
                for mh in range(4):
                    spec[ri, pl.ds(j * PEERS, PEERS), pl.ds(mh * 128, 128)] = msg32[
                        pl.ds(ri * 8 + mh * 2 + j, PEERS, stride=16), :
                    ]
        for s in range(SEQS):
            rows, rows_im = pl.ds(s * RES, RES), pl.ds((2 + s) * RES, RES)
            f_re = wide[0, rows, :] + wide[1, rows_im, :]
            f_im = wide[0, rows_im, :] - wide[1, rows, :]
            lhs_hi[pl.ds(base(chl, 0, s), RES), :] = (f_re * spec[0] - f_im * spec[1]).astype(BF16)
            lhs_hi[pl.ds(base(chl, 1, s), RES), :] = (f_re * spec[1] + f_im * spec[0]).astype(BF16)
        for which in range(2):
            wide[which] = inner(which, channel)
        for s in range(SEQS):
            rows, rows_im = pl.ds(s * RES, RES), pl.ds((2 + s) * RES, RES)
            b_re = wide[0, rows, :] - wide[1, rows_im, :]
            b_im = wide[0, rows_im, :] + wide[1, rows, :]
            re_hi, re_lo = split(b_re * tw[0] - b_im * tw[1])
            im_hi, im_lo = split(b_im * tw[0] + b_re * tw[1])
            signal = dot(
                last[...], jnp.concatenate([re_hi, im_hi, re_lo, im_lo, re_hi, im_hi], axis=0)
            )
            for bh in range(4):
                msg32[pl.ds(s * 4 + bh, PEERS, stride=8), :] = signal[:, bh * 128 : (bh + 1) * 128]
        bsend[chl] = msg32[pl.ds(0, PEERS * 8), :].reshape(PEERS, 8, 128).astype(BF16)
        exchange(bsend.at[chl], brecv.at[chl], 3 + chl)

    def quarter_copy(chl, k):
        return pltpu.make_async_remote_copy(
            src_ref=mbuf.at[chl, (y + k) % RING],
            dst_ref=gbuf.at[zl, chl, RING - k],
            send_sem=y_send.at[chl, k - 1],
            recv_sem=y_recv.at[chl],
            device_id={"tensor": ring + (y + k) % RING, "context": me},
            device_id_type=MESH,
        )

    def mix(chl):
        wait_all(brecv.at[chl], a2a_recv.at[3 + chl])
        msg32[pl.ds(0, PEERS * 8), :] = brecv[chl].astype(F32).reshape(PEERS * 8, 128)
        for bh in range(4):
            pieces = []
            for s in range(SEQS):
                rows = pl.ds(s * LOCAL_CH + chl, PEERS, stride=2)
                conv = msg32[pl.ds(s * 4 + bh, PEERS, stride=8), :]
                pieces.append(gate32[bh, rows, :] * (conv + skipped[bh, rows, :]))
            for s in range(SEQS):
                mbuf[chl, bh, s] = pieces[s].astype(BF16)
        for k in (2, 1, 3):
            quarter_copy(chl, k).start()
        gbuf[zl, chl, 0] = mbuf[chl, y]

    def z_copy(origin, part, slot, target):
        others = pl.ds(1, RING - 1)
        ref = (
            gbuf.at[origin, 0, 0],
            gbuf.at[origin, 0, others],
            gbuf.at[origin, 1, 0],
            gbuf.at[origin, 1, others, 0],
            gbuf.at[origin, 1, others, 1],
        )[part]
        return pltpu.make_async_remote_copy(
            src_ref=ref,
            dst_ref=ref,
            send_sem=z_send.at[part, slot],
            recv_sem=z_recv.at[part, origin],
            device_id={"tensor": target, "context": me},
            device_id_type=MESH,
        )

    inner_chip = (zl == 1) | (zl == 2)
    partner = (zl + 1 - 2 * (zl % 2), (zl + 2) % RING, RING - 1 - zl)

    def z_sends(part, visit):
        for k in (2, 1):

            @pl.when(zl < RING - k)
            def _():
                visit(z_copy(zl, part, 2 * k - 2, t + k * RING))

            @pl.when(zl >= k)
            def _():
                visit(z_copy(zl, part, 2 * k - 1, t - k * RING))

    def pass_on(part):
        return z_copy(partner[1], part, 4, t + (2 * zl - 3) * RING)

    def wait_quarters(chl):
        view = gbuf.at[0, chl, pl.ds(0, RING - 1)]
        pltpu.make_async_copy(view, view, y_recv.at[chl]).wait()

    def z_wait(part, k):
        z_copy(partner[k - 1], part, 0, t).wait_recv()
        if k == 2:

            @pl.when(inner_chip)
            def _():
                pass_on(part).start()

    def tokens_of(z, chl, s):
        return gbuf[z, chl, :, s].astype(F32).reshape(128, 128).T.astype(BF16)

    def weights_of(z, chl, column):
        return jnp.concatenate(
            [wg[column, z * RING + (y + r) % RING, chl] for r in range(RING)], axis=0
        )

    def project(chl, s, items):
        lhs = jnp.concatenate([tokens_of(z, chl, s) for z in items], axis=1)

        def columns(column):
            return dot(lhs, jnp.concatenate([weights_of(z, chl, column) for z in items], axis=0))

        return columns

    def result_copy(s, k):
        column = (y + k) % RING
        return pltpu.make_async_remote_copy(
            src_ref=osend.at[s, column],
            dst_ref=out_ref.at[s, pl.ds(y * 128, 128), :],
            send_sem=o_send.at[s, k - 1],
            recv_sem=o_recv.at[s, k - 1],
            device_id={"tensor": ring + column, "context": me},
            device_id_type=MESH,
        )

    def own_result(s):
        return pltpu.make_async_copy(
            osend.at[s, y], out_ref.at[s, pl.ds(y * 128, 128), :], o_own.at[s]
        )

    def start(part):
        z_sends(part, lambda c: c.start())

    mix(0)
    start(0)
    wait_quarters(0)
    start(1)
    mix(1)
    start(2)
    z_wait(0, 2)
    wait_quarters(1)
    start(3)
    start(4)
    z_wait(1, 2)
    z_wait(2, 2)
    z_wait(0, 1)
    z_wait(1, 1)
    for c in w_copies:
        c.wait_recv()
    for s in range(SEQS):
        near = project(0, s, (zl, partner[0]))
        for column in range(RING):
            acc[s, column] = near(column)
    z_wait(3, 2)
    z_wait(0, 3)
    z_wait(1, 3)
    for s in range(SEQS):
        far = project(0, s, (partner[1], partner[2]))
        for column in range(RING):
            acc[s, column] += far(column)
    z_wait(4, 2)
    z_wait(2, 1)
    z_wait(2, 3)
    for s in range(SEQS):
        z_wait(3 + s, 1)
        near = project(1, s, (zl, partner[0]))
        for column in range(RING):
            acc[s, column] += near(column)
        z_wait(3 + s, 3)
        far = project(1, s, (partner[1], partner[2]))
        for k in (2, 1, 3, 0):
            column = (y + k) % RING
            osend[s, column] = (acc[s, column] + far(column)).astype(BF16)
            if k:
                result_copy(s, k).start()
            else:
                own_result(s).start()
    for s in range(SEQS):
        own_result(s).wait()
        for k in range(1, RING):
            result_copy(s, k).wait_recv()

    for part in range(5):
        z_sends(part, lambda c: c.wait_send())

        @pl.when(inner_chip)
        def _():
            pass_on(part).wait_send()

    for k in range(1, RING):
        w_copies[k - 1].wait_send()
        for s in range(SEQS):
            result_copy(s, k).wait_send()
        for chl in range(2):
            quarter_copy(chl, k).wait_send()
    for i, buf in enumerate((sseq, sfilt.at[0], sfilt.at[1], bsend.at[0], bsend.at[1])):
        wait_all(buf, a2a_send.at[i])


def local(sequence, gate, skip, filter_spectrum, out_weight):
    first, last, dft, twiddle = tables()
    rows = filter_spectrum.reshape(2, LOCAL_CH, 2, 4, 128).transpose(0, 1, 3, 2, 4).reshape(-1, 128)
    hbm = pl.BlockSpec(memory_space=pl.ANY)
    return pl.pallas_call(
        kernel,
        out_shape=jax.ShapeDtypeStruct((SEQS, BLOCK, COLS), BF16),
        in_specs=[hbm] * 9,
        out_specs=hbm,
        scratch_shapes=[
            pltpu.VMEM((SEQS, LOCAL_CH, BLOCK), BF16),
            pltpu.VMEM((PEERS * 32, 128), F32),
            pltpu.VMEM((1, LOCAL_CH), F32),
            pltpu.VMEM((2 * RES, 2 * PEERS), BF16),
            pltpu.VMEM((PEERS, 6 * RES), BF16),
            pltpu.VMEM((SEQS, LOCAL_CH, BLOCK), BF16),
            pltpu.VMEM((RING * RING * LOCAL_CH, COLS), BF16),
            pltpu.VMEM((4, BLOCK, BLOCK), BF16),
            pltpu.VMEM((2, RES, BLOCK), F32),
            pltpu.VMEM((4, SEQS * LOCAL_CH + 8, 128), F32),
            pltpu.VMEM((4, SEQS * LOCAL_CH + 8, 128), F32),
            pltpu.VMEM((4, SEQS * LOCAL_CH + 8, 128), F32),
            pltpu.VMEM((2, RING * RING * LOCAL_CH + 8, 128), F32),
            pltpu.VMEM((PEERS * 16 + 16, 128), F32),
            pltpu.VMEM((PEERS, 16, 128), BF16),
            pltpu.VMEM((PEERS, 16, 128), BF16),
            pltpu.VMEM((2, PEERS, 16, 128), BF16),
            pltpu.VMEM((2, PEERS, 16, 128), BF16),
            pltpu.VMEM((2, RES, BLOCK), F32),
            pltpu.VMEM((2, 4 * RES, BLOCK), F32),
            pltpu.VMEM((8 * RES, BLOCK), BF16),
            pltpu.VMEM((8 * RES, BLOCK), BF16),
            pltpu.VMEM((2, PEERS, 8, 128), BF16),
            pltpu.VMEM((2, PEERS, 8, 128), BF16),
            pltpu.VMEM((2, RING, SEQS, PEERS, 128), BF16),
            pltpu.VMEM((RING, 2, RING, SEQS, PEERS, 128), BF16),
            pltpu.VMEM((RING, RING * RING, 2, PEERS, COLS), BF16),
            pltpu.VMEM((SEQS, RING, 128, COLS), F32),
            pltpu.VMEM((SEQS, RING, 128, COLS), BF16),
            pltpu.SemaphoreType.DMA((9,)),
            pltpu.SemaphoreType.DMA((5,)),
            pltpu.SemaphoreType.DMA((5,)),
            pltpu.SemaphoreType.DMA((RING - 1,)),
            pltpu.SemaphoreType.DMA((RING - 1,)),
            pltpu.SemaphoreType.DMA((2, RING - 1)),
            pltpu.SemaphoreType.DMA((2,)),
            pltpu.SemaphoreType.DMA((5, 5)),
            pltpu.SemaphoreType.DMA((5, RING)),
            pltpu.SemaphoreType.DMA((SEQS, RING - 1)),
            pltpu.SemaphoreType.DMA((SEQS, RING - 1)),
            pltpu.SemaphoreType.DMA((SEQS,)),
            pltpu.SemaphoreType.REGULAR,
        ],
        compiler_params=pltpu.CompilerParams(
            collective_id=0, has_side_effects=True, vmem_limit_bytes=62 * 1024 * 1024
        ),
    )(
        sequence, rows, skip.reshape(1, LOCAL_CH), jnp.asarray(first), jnp.asarray(last),
        gate, out_weight, jnp.asarray(dft), jnp.asarray(twiddle),
    )


def solution(mesh):
    in_specs = (
        P(None, "tensor", "context"),
        P(None, "tensor", "context"),
        P("tensor"),
        P(None, "tensor", "context", None),
        P(None, "tensor"),
    )
    out_specs = P(None, "context", "tensor")
    return jax.shard_map(local, mesh=mesh, in_specs=in_specs, out_specs=out_specs, check_vma=False)
```
